128 devices in a mesh: row: 8 (over z, core), col: 16 (over y, x).
Axes of the slice: x: 4, y: 4, z: 4, core: 2. Of those that a mesh axis runs over, the one named last changes fastest.
Arguments:
- vectors: bfloat16 [32, 32, 16, 256], P('row', 'col'), may hold values from -6 to 6
- near_blocks: bfloat16 [32, 32, 9, 256, 256], P('row', 'col'), may hold values from -0.125 to 0.125
- near_mask: int32 [32, 32, 8], P('row', 'col'), may hold values 0 or 1
- far_mask: int32 [32, 32, 16], P('row', 'col'), may hold values 0 or 1
- leaf_basis: bfloat16 [32, 32, 256, 64], P('row', 'col'), may hold values from -0.375 to 0.375
- far_transfer: bfloat16 [24, 64, 64], replicated, may hold values from -0.15625 to 0.15625
- coarse_basis: bfloat16 [32, 32, 64, 256], P('row', 'col'), may hold values from -0.25 to 0.25
- coarse_list: int32 [128, 8], P(('row', 'col')), may hold values from 0 to 127, as said below
- coarse_transfer: float32 [128, 8, 256, 256], P(('row', 'col')), may hold values from -0.125 to 0.125
Outputs:
- applied: float32 [32, 32, 16, 256], P('row', 'col')
The draws below stay inside these ranges and needn't reach their ends.
Inputs may be any that keep to these rules, and one draw needn't show every extreme that they name: `coarse_list`: each row lists 8 distinct coarse clusters, never its own; cluster d is the device with row index d // 16 and col index d % 16. Every listed cluster's row index and col index each differ from those of d by at most 2.
All inputs are finite; a program needn't handle non-finite values. No bound on the sum of `near_mask` or of `far_mask` on one device may be relied on, other than what follows from the above.
Results may differ from the reference program's by a relative error of at most 0.003.
Values may be sent and summed in bfloat16 or wider, within the bound.
A program may use at most 64 MiB of HBM per device.

```python
import jax
import jax.numpy as jnp
from jax import lax

LEAF = 256
RHS = 16
RANK = 64
COARSE = 256
FAR2 = 8
LX = 4
LY = 2
GRID_X = 32
GRID_Y = 32
DEV_COUNT = 128
N_ROW = 8
N_COL = 16


def draw_coarse_list(key, part):
    key = jax.random.fold_in(key, 11)
    cluster = jnp.arange(DEV_COUNT, dtype=jnp.int32)
    row_of = cluster // N_COL
    col_of = cluster % N_COL
    row_gap = jnp.abs(row_of[:, None] - row_of[None, :])
    col_gap = jnp.abs(col_of[:, None] - col_of[None, :])
    allowed = (row_gap <= 2) & (col_gap <= 2) & (cluster[:, None] != cluster[None, :])
    scores = jax.random.randint(key, (DEV_COUNT, DEV_COUNT), 0, 2 ** 20) * DEV_COUNT + cluster[None, :]
    scores = jnp.where(allowed, scores, -1)
    return lax.top_k(scores, FAR2)[1].astype(jnp.int32)


def with_ends(array, stream_key, least, high):
    extent = array.shape
    place = [jax.random.randint(jax.random.fold_in(stream_key, axis), (), 0, extent[axis]) for axis in range(len(extent))]
    array = array.at[tuple(place)].set(least)
    longest = extent.index(max(extent))
    place[longest] = (place[longest] + 1) % extent[longest]
    return array.at[tuple(place)].set(high)


def levels(stream_key, shape, cuts, least, high):
    def one(dim, parts):
        draws = jax.random.uniform(jax.random.fold_in(jax.random.fold_in(stream_key, 6), dim), (parts,), jnp.float32, least / len(cuts), high / len(cuts))
        return jnp.repeat(jnp.exp(draws), shape[dim] // parts).reshape((-1,) + (1,) * (len(shape) - dim - 1))

    gain = one(*cuts[0])
    for cut in cuts[1:]:
        gain = gain * one(*cut)
    return gain


def centred(stream_key, dims, deviation, most, cuts=(), kind=jnp.bfloat16):
    entries = deviation * jax.random.normal(stream_key, dims, jnp.float32)
    if cuts:
        entries = entries * levels(stream_key, dims, cuts, -0.22, 0.18)
    return jnp.clip(entries, -most, most).astype(kind)


def setup_inputs(seed: int = 0) -> dict:
    streams_of = jax.random.split(jax.random.key(seed), 10)
    vectors = centred(streams_of[0], (GRID_X, GRID_Y, RHS, LEAF), 1.0, 6.0, ((0, 8), (1, 16)))
    near_blocks = centred(streams_of[1], (GRID_X, GRID_Y, 9, LEAF, LEAF), (9 * LEAF) ** -0.5, 0.125, ((0, 8), (1, 16)))
    near_mask = with_ends((jax.random.randint(streams_of[2], (GRID_X, GRID_Y, 8), 0, 2) < 1).astype(jnp.int32), jax.random.fold_in(streams_of[2], 1), 0, 1)
    far_mask = with_ends((jax.random.randint(streams_of[3], (GRID_X, GRID_Y, 16), 0, 4) < 3).astype(jnp.int32), jax.random.fold_in(streams_of[3], 1), 0, 1)
    leaf_basis = centred(streams_of[4], (GRID_X, GRID_Y, LEAF, RANK), LEAF ** -0.5, 0.375, ((0, 8), (1, 16)))
    far_transfer = centred(streams_of[5], (24, RANK, RANK), (24 * RANK) ** -0.5, 0.15625)
    coarse_basis = centred(streams_of[6], (GRID_X, GRID_Y, RANK, COARSE), (RANK * LX * LY) ** -0.5, 0.25, ((0, 8), (1, 16)))
    coarse_list = draw_coarse_list(jax.random.fold_in(streams_of[9], 71), 0)
    coarse_transfer = centred(streams_of[8], (DEV_COUNT, FAR2, COARSE, COARSE), (COARSE * FAR2) ** -0.5, 0.125, ((0, 128),), jnp.float32)
    return dict(vectors=vectors, near_blocks=near_blocks, near_mask=near_mask, far_mask=far_mask, leaf_basis=leaf_basis, far_transfer=far_transfer, coarse_basis=coarse_basis, coarse_list=coarse_list, coarse_transfer=coarse_transfer)


NEAR_OFFSETS = [(step_a, step_b) for step_a in (-1, 0, 1) for step_b in (-1, 0, 1)]
FAR_OFFSETS = [(step_a, step_b) for step_a in (-2, -1, 0, 1, 2) for step_b in (-2, -1, 0, 1, 2) if (step_a, step_b) != (0, 0)]


def near_live(near_mask):
    ones_col = jnp.ones(near_mask.shape[:2] + (1,), jnp.int32)
    return jnp.concatenate([near_mask[:, :, :4], ones_col, near_mask[:, :, 4:]], axis=2)


def far_weights(near_mask, far_mask):
    columns = []
    cycle_one = 0
    cycle_two = 0
    for step_a, step_b in FAR_OFFSETS:
        if max(abs(step_a), abs(step_b)) == 1:
            columns.append(1 - near_mask[:, :, cycle_one])
            cycle_one += 1
        else:
            columns.append(far_mask[:, :, cycle_two])
            cycle_two += 1
    return jnp.stack(columns, axis=2)


def reference(vectors, near_blocks, near_mask, far_mask, leaf_basis, far_transfer, coarse_basis, coarse_list, coarse_transfer):
    live = near_live(near_mask).astype(jnp.float32)
    vec_pad = jnp.pad(vectors.astype(jnp.float32), ((1, 1), (1, 1), (0, 0), (0, 0)))

    def near_row(index):
        blocks = near_blocks[index].astype(jnp.float32)
        rows = lax.dynamic_slice_in_dim(vec_pad, index, 3, 0)
        stacked = jnp.stack([rows[1 + step_a, 1 + step_b:1 + step_b + GRID_Y] for step_a, step_b in NEAR_OFFSETS], axis=1)
        stacked = stacked * live[index][:, :, None, None]
        return jnp.einsum("ysrl,yslm->yrm", stacked, blocks)

    near = lax.map(near_row, jnp.arange(GRID_X))
    coeffs = jnp.einsum("xyrl,xylk->xyrk", vectors.astype(jnp.float32), leaf_basis.astype(jnp.float32)).astype(jnp.bfloat16)
    coeff_pad = jnp.pad(coeffs.astype(jnp.float32), ((2, 2), (2, 2), (0, 0), (0, 0)))
    weight = far_weights(near_mask, far_mask).astype(jnp.float32)
    stacked_far = jnp.stack([coeff_pad[2 + step_a:2 + step_a + GRID_X, 2 + step_b:2 + step_b + GRID_Y] for step_a, step_b in FAR_OFFSETS], axis=2)
    stacked_far = stacked_far * weight[:, :, :, None, None]
    local_leaf = jnp.einsum("xyors,osk->xyrk", stacked_far, far_transfer.astype(jnp.float32))
    blocked = coeffs.astype(jnp.float32).reshape(N_ROW, LX, N_COL, LY, RHS, RANK)
    basis_blocked = coarse_basis.astype(jnp.float32).reshape(N_ROW, LX, N_COL, LY, RANK, COARSE)
    coarse = jnp.einsum("axbyrk,axbykj->abrj", blocked, basis_blocked).reshape(N_ROW * N_COL, RHS, COARSE)
    picked = coarse[coarse_list]
    coarse_local = jnp.einsum("dfrs,dfsk->drk", picked, coarse_transfer, precision=lax.Precision.HIGHEST).astype(jnp.bfloat16)
    coarse_local = coarse_local.astype(jnp.float32).reshape(N_ROW, N_COL, RHS, COARSE)
    downward = jnp.einsum("abrj,axbykj->axbyrk", coarse_local, basis_blocked).reshape(GRID_X, GRID_Y, RHS, RANK)
    local_all = (local_leaf + downward).astype(jnp.bfloat16)
    far_part = jnp.einsum("xyrk,xylk->xyrl", local_all.astype(jnp.float32), leaf_basis.astype(jnp.float32))
    return near + far_part
```

```python
import jax
import jax.numpy as jnp
from jax import lax
from jax.experimental import pallas as pl
from jax.experimental.pallas import tpu as pltpu
from jax.sharding import PartitionSpec as P

MESH = pl.DeviceIdType.MESH
LX, LY, RHS, LEAF, RANK, COARSE, FAR2 = 4, 2, 16, 256, 64, 256, 8
N_ROW, N_COL = 8, 16
NEAR_OFFSETS = [(a, b) for a in (-1, 0, 1) for b in (-1, 0, 1)]
FAR_OFFSETS = [(a, b) for a in range(-2, 3) for b in range(-2, 3) if (a, b) != (0, 0)]
RING1 = [(a, b) for a, b in NEAR_OFFSETS if (a, b) != (0, 0)]
RING2 = FAR_OFFSETS
BF16, F32 = jnp.bfloat16, jnp.float32


def dot(lhs, rhs):
    return lax.dot_general(lhs, rhs, (((1,), (0,)), ((), ())), preferred_element_type=F32)


def dot_t(lhs, rhs):
    return lax.dot_general(lhs, rhs, (((1,), (1,)), ((), ())), preferred_element_type=F32)


def halo_part(a, b, width):
    src, size, dst = [], [], []
    for step, own in ((a, LX), (b, LY)):
        size.append(own if step == 0 else width)
        src.append(own - width if step == 1 else 0)
        dst.append({-1: width + own, 0: width, 1: 0}[step])
    return src, size, dst


def kernel(
    vec_hbm, near_hbm, near_mask_hbm, far_mask_hbm, leaf_hbm, transfer_hbm, cbasis_hbm, clist_hbm, ctrans_hbm,
    out_ref,
    vecs, coef, coarse, nblk, leafb, ftr, cbasis, ctr, ctr_hi, ctr_lo, near_acc, weights,
    near_mask, far_mask, clist,
    near_sem, load_sem, vec_send, vec_recv, coef_send, coef_recv, coarse_send, coarse_recv,
):
    row = lax.axis_index("row")
    col = lax.axis_index("col")

    def at(a, b):
        return (row + a, col + b)

    def when_there(a, b):
        r, c = at(a, b)
        return pl.when((r >= 0) & (r < N_ROW) & (c >= 0) & (c < N_COL))

    load_leaf = pltpu.make_async_copy(leaf_hbm, leafb, load_sem.at[0])
    load_leaf.start()
    load_cbasis = pltpu.make_async_copy(cbasis_hbm, cbasis, load_sem.at[1])
    load_cbasis.start()

    vecs[...] = jnp.zeros_like(vecs)
    coef[...] = jnp.zeros_like(coef)

    barrier = pltpu.get_barrier_semaphore()
    for a, b in RING2:
        @when_there(a, b)
        def _():
            pl.semaphore_signal(barrier, inc=1, device_id=at(a, b), device_id_type=MESH)

    load_vec = pltpu.make_async_copy(vec_hbm, vecs.at[pl.ds(1, LX), pl.ds(1, LY)], load_sem.at[2])
    load_vec.start()
    load_small = []
    for k, (src, dst) in enumerate(((near_mask_hbm, near_mask), (far_mask_hbm, far_mask), (clist_hbm, clist))):
        load_small.append(pltpu.make_async_copy(src, dst, load_sem.at[5 + k]))
        load_small[-1].start()
    load_ctr = pltpu.make_async_copy(ctrans_hbm, ctr, load_sem.at[3])
    load_near = []
    for p in range(LX * LY):
        load_near.append(pltpu.make_async_copy(near_hbm.at[p // LY, p % LY], nblk.at[p], near_sem.at[p]))
        load_near[-1].start()
        if p == 0:
            load_ctr.start()
    load_ftr = pltpu.make_async_copy(transfer_hbm, ftr, load_sem.at[4])
    load_ftr.start()

    row_count = jnp.minimum(row, 2) + jnp.minimum(N_ROW - 1 - row, 2) + 1
    col_count = jnp.minimum(col, 2) + jnp.minimum(N_COL - 1 - col, 2) + 1
    pl.semaphore_wait(barrier, row_count * col_count - 1)

    def vec_copy(a, b):
        src, size, dst = halo_part(a, b, 1)
        k = RING1.index((a, b))
        return pltpu.make_async_remote_copy(
            src_ref=vecs.at[pl.ds(1 + src[0], size[0]), pl.ds(1 + src[1], size[1])],
            dst_ref=vecs.at[pl.ds(dst[0], size[0]), pl.ds(dst[1], size[1])],
            send_sem=vec_send.at[k], recv_sem=vec_recv.at[k], device_id=at(a, b), device_id_type=MESH,
        )

    def coef_copy(a, b):
        src, size, dst = halo_part(a, b, 2)
        k = RING1.index((a, b))
        return pltpu.make_async_remote_copy(
            src_ref=coef.at[pl.ds(2 + src[0], size[0]), pl.ds(2 + src[1], size[1])],
            dst_ref=coef.at[pl.ds(dst[0], size[0]), pl.ds(dst[1], size[1])],
            send_sem=coef_send.at[k], recv_sem=coef_recv.at[k], device_id=at(a, b), device_id_type=MESH,
        )

    def coarse_copy(a, b):
        slot = (2 - a) * 5 + 2 - b
        return pltpu.make_async_remote_copy(
            src_ref=coarse.at[12], dst_ref=coarse.at[slot],
            send_sem=coarse_send.at[slot], recv_sem=coarse_recv.at[slot], device_id=at(a, b), device_id_type=MESH,
        )

    load_vec.wait()
    for a, b in RING1:
        @when_there(a, b)
        def _():
            vec_copy(a, b).start()

    load_leaf.wait()
    for p in range(LX * LY):
        i, j = p // LY, p % LY
        coef[2 + i, 2 + j] = dot_t(vecs[1 + i, 1 + j], leafb[i, j]).astype(BF16)
    for a, b in RING1:
        @when_there(a, b)
        def _():
            coef_copy(a, b).start()

    load_cbasis.wait()
    own = jnp.zeros((RHS, COARSE), F32)
    for p in range(LX * LY):
        i, j = p // LY, p % LY
        own += dot(coef[2 + i, 2 + j], cbasis[i, j])
    coarse[12] = own
    for a, b in RING2:
        @when_there(a, b)
        def _():
            coarse_copy(a, b).start()

    for copy in load_small:
        copy.wait()
    for o, (a, b) in enumerate(FAR_OFFSETS):
        ring = [x for x in FAR_OFFSETS if (max(abs(x[0]), abs(x[1])) == 1) == (max(abs(a), abs(b)) == 1)].index((a, b))
        for p in range(LX * LY):
            i, j = p // LY, p % LY
            if max(abs(a), abs(b)) == 1:
                w = 1 - near_mask[i, j, ring]
            else:
                w = far_mask[i, j, ring]
            weights[o, p] = jnp.full((RHS, RANK), w.astype(F32), F32).astype(BF16)

    def near_term(p, s):
        i, j = p // LY, p % LY
        a, b = NEAR_OFFSETS[s]
        lhs = vecs[1 + i + a, 1 + j + b]
        if s != 4:
            live = near_mask[i, j, s if s < 4 else s - 1]
            lhs = lhs * jnp.full((RHS, LEAF), live.astype(F32), F32).astype(BF16)
        return dot(lhs, nblk[p, s])

    def inside(p, s):
        a, b = NEAR_OFFSETS[s]
        return 0 <= p // LY + a < LX and 0 <= p % LY + b < LY

    for p in range(LX * LY):
        load_near[p].wait()
        near_acc[p] = sum(near_term(p, s) for s in range(9) if inside(p, s))

    load_ctr.wait()
    for f in range(FAR2):
        whole = ctr[f]
        hi = whole.astype(BF16)
        ctr_hi[f] = hi
        ctr_lo[f] = (whole - hi.astype(F32)).astype(BF16)

    for a, b in RING1:
        @when_there(a, b)
        def _():
            vec_copy(-a, -b).wait_recv()
    for p in range(LX * LY):
        outer = [s for s in range(9) if not inside(p, s)]
        if outer:
            near_acc[p] += sum(near_term(p, s) for s in outer)

    load_ftr.wait()
    for a, b in RING1:
        @when_there(a, b)
        def _():
            coef_copy(-a, -b).wait_recv()
    local = jnp.zeros((LX * LY * RHS, RANK), F32)
    for o, (a, b) in enumerate(FAR_OFFSETS):
        lhs = coef[2 + a : 2 + a + LX, 2 + b : 2 + b + LY].reshape(LX * LY, RHS, RANK) * weights[o]
        local += dot(lhs.reshape(LX * LY * RHS, RANK), ftr[o])

    for a, b in RING1:
        @when_there(a, b)
        def _():
            vec_copy(a, b).wait_send()
            coef_copy(a, b).wait_send()
    for a, b in RING2:
        @when_there(a, b)
        def _():
            coarse_copy(a, b).wait_send()
    for a, b in RING2:
        @when_there(a, b)
        def _():
            coarse_copy(-a, -b).wait_recv()

    total = jnp.zeros((RHS, COARSE), F32)
    for f in range(FAR2):
        listed = clist[0, f]
        slot = (listed // N_COL - row + 2) * 5 + listed % N_COL - col + 2
        whole = coarse[jnp.clip(slot, 0, 24)]
        hi = whole.astype(BF16)
        lo = (whole - hi.astype(F32)).astype(BF16)
        total += dot(hi, ctr_hi[f]) + (dot(lo, ctr_hi[f]) + dot(hi, ctr_lo[f]))
    coarse_local = total.astype(BF16)
    for p in range(LX * LY):
        i, j = p // LY, p % LY
        down = dot_t(coarse_local, cbasis[i, j])
        both = (local[p * RHS : (p + 1) * RHS] + down).astype(BF16)
        out_ref[i, j] = near_acc[p] + dot(both, leafb[i, j])


def per_device(vectors, near_blocks, near_mask, far_mask, leaf_basis, far_transfer, coarse_basis, coarse_list, coarse_transfer):
    any_ = pl.BlockSpec(memory_space=pltpu.HBM)
    vmem = pl.BlockSpec(memory_space=pltpu.VMEM)
    dma = pltpu.SemaphoreType.DMA
    operands = [
        pltpu.with_memory_space_constraint(x, pltpu.HBM)
        for x in (
            vectors, near_blocks, near_mask, far_mask, leaf_basis.swapaxes(2, 3), far_transfer, coarse_basis, coarse_list,
            coarse_transfer[0],
        )
    ]
    return pl.pallas_call(
        kernel,
        out_shape=jax.ShapeDtypeStruct((LX, LY, RHS, LEAF), F32),
        in_specs=[any_] * 9,
        out_specs=vmem,
        scratch_shapes=[
            pltpu.VMEM((LX + 2, LY + 2, RHS, LEAF), BF16),
            pltpu.VMEM((LX + 4, LY + 4, RHS, RANK), BF16),
            pltpu.VMEM((25, RHS, COARSE), F32),
            pltpu.VMEM((LX * LY, 9, LEAF, LEAF), BF16),
            pltpu.VMEM((LX, LY, RANK, LEAF), BF16),
            pltpu.VMEM((24, RANK, RANK), BF16),
            pltpu.VMEM((LX, LY, RANK, COARSE), BF16),
            pltpu.VMEM((FAR2, COARSE, COARSE), F32),
            pltpu.VMEM((FAR2, COARSE, COARSE), BF16),
            pltpu.VMEM((FAR2, COARSE, COARSE), BF16),
            pltpu.VMEM((LX * LY, RHS, LEAF), F32),
            pltpu.VMEM((24, LX * LY, RHS, RANK), BF16),
            pltpu.SMEM((LX, LY, 8), jnp.int32),
            pltpu.SMEM((LX, LY, 16), jnp.int32),
            pltpu.SMEM((1, FAR2), jnp.int32),
            dma((LX * LY,)),
            dma((8,)),
            dma((8,)),
            dma((8,)),
            dma((8,)),
            dma((8,)),
            dma((25,)),
            dma((25,)),
        ],
        compiler_params=pltpu.CompilerParams(
            collective_id=0, has_side_effects=True, vmem_limit_bytes=40 * 1024 * 1024
        ),
    )(*operands)


def solution(mesh):
    placed = (
        P("row", "col", None, None),
        P("row", "col", None, None, None),
        P("row", "col", None),
        P("row", "col", None),
        P("row", "col", None, None),
        P(),
        P("row", "col", None, None),
        P(("row", "col"), None),
        P(("row", "col"), None, None, None),
    )
    return jax.shard_map(
        per_device, mesh=mesh, in_specs=placed, out_specs=P("row", "col", None, None), check_vma=False
    )
```

```python
import functools

import jax
import jax.numpy as jnp
from jax import lax
from jax.experimental import pallas as pl
from jax.experimental.pallas import tpu as pltpu
from jax.sharding import PartitionSpec as P

MESH = pl.DeviceIdType.MESH
LX, LY, RHS, LEAF, RANK, COARSE, FAR2 = 4, 2, 16, 256, 64, 256, 8
N_ROW, N_COL = 8, 16
NEAR_OFFSETS = [(a, b) for a in (-1, 0, 1) for b in (-1, 0, 1)]
FAR_OFFSETS = [(a, b) for a in range(-2, 3) for b in range(-2, 3) if (a, b) != (0, 0)]
RING1 = [(a, b) for a, b in NEAR_OFFSETS if (a, b) != (0, 0)]
COLS = [(0, -2), (0, 2), (0, -1), (0, 1)]
ROWS = [(-2, 0), (2, 0), (-1, 0), (1, 0)]
CORNERS = [(-1, -1), (-1, 1), (1, -1), (1, 1)]
PARTNERS = COLS + ROWS + CORNERS
NEAR_FIRST = 6
PLACE = {0: 0, -2: 1, -1: 2, 1: 3, 2: 4}
BF16, F32 = jnp.bfloat16, jnp.float32


def dot(lhs, rhs):
    return lax.dot_general(lhs, rhs, (((1,), (0,)), ((), ())), preferred_element_type=F32)


def dot_t(lhs, rhs):
    return lax.dot_general(lhs, rhs, (((1,), (1,)), ((), ())), preferred_element_type=F32)


def halo_part(a, b, width):
    src, size, dst = [], [], []
    for step, own in ((a, LX), (b, LY)):
        size.append(own if step == 0 else width)
        src.append(own - width if step == 1 else 0)
        dst.append({-1: width + own, 0: width, 1: 0}[step])
    return src, size, dst


def kernel(
    vec_hbm, near_hbm, near_mask_hbm, far_mask_hbm, leaf_hbm, transfer_hbm, cbasis_hbm, clist_hbm, ctrans_hbm,
    out_ref,
    vecs, coef, coarse, nblk, leafb, ftr, cbasis, ctr, ctr_hi, ctr_lo, near_acc, weights,
    near_mask, far_mask, clist,
    near_sem, load_sem, vec_send, vec_recv, coef_send, coef_recv, coarse_send, coarse_recv,
):
    row = lax.axis_index("row")
    col = lax.axis_index("col")

    def at(a, b):
        return (row + a, col + b)

    there = {}
    for a, b in PARTNERS:
        r, c = at(a, b)
        there[a, b] = (r >= 0) & (r < N_ROW) & (c >= 0) & (c < N_COL)

    def each(offsets, step):
        for a, b in offsets:
            pl.when(there[a, b])(functools.partial(step, a, b))

    load_vec = pltpu.make_async_copy(vec_hbm, vecs.at[pl.ds(1, LX), pl.ds(1, LY)], load_sem.at[2])
    load_vec.start()
    load_leaf = pltpu.make_async_copy(leaf_hbm, leafb, load_sem.at[0])
    load_leaf.start()
    load_cbasis = pltpu.make_async_copy(cbasis_hbm, cbasis, load_sem.at[1])
    load_cbasis.start()

    for ref, width, last in ((vecs, 1, LEAF), (coef, 2, RANK)):
        edge = jnp.zeros((width, LY + 2 * width, RHS, last), BF16)
        side = jnp.zeros((LX, width, RHS, last), BF16)
        ref[0:width] = edge
        ref[width + LX : 2 * width + LX] = edge
        ref[width : width + LX, 0:width] = side
        ref[width : width + LX, width + LY : 2 * width + LY] = side
    coarse[2, 1:5] = jnp.zeros((4, RHS, COARSE), F32)

    barrier = pltpu.get_barrier_semaphore()
    each(PARTNERS, lambda a, b: pl.semaphore_signal(barrier, inc=1, device_id=at(a, b), device_id_type=MESH))

    load_small = []
    for k, (src, dst) in enumerate(((near_mask_hbm, near_mask), (far_mask_hbm, far_mask), (clist_hbm, clist))):
        load_small.append(pltpu.make_async_copy(src, dst, load_sem.at[5 + k]))
        load_small[-1].start()
    load_ctr = pltpu.make_async_copy(ctrans_hbm, ctr, load_sem.at[3])
    load_near = []
    for p in range(LX * LY):
        load_near.append(pltpu.make_async_copy(near_hbm.at[p // LY, p % LY], nblk.at[p], near_sem.at[p]))
        load_near[-1].start()
        if p == 0:
            load_ctr.start()
    load_ftr = pltpu.make_async_copy(transfer_hbm, ftr, load_sem.at[4])
    load_ftr.start()

    def vec_copy(a, b):
        src, size, dst = halo_part(a, b, 1)
        k = RING1.index((a, b))
        return pltpu.make_async_remote_copy(
            src_ref=vecs.at[pl.ds(1 + src[0], size[0]), pl.ds(1 + src[1], size[1])],
            dst_ref=vecs.at[pl.ds(dst[0], size[0]), pl.ds(dst[1], size[1])],
            send_sem=vec_send.at[k], recv_sem=vec_recv.at[k], device_id=at(a, b), device_id_type=MESH,
        )

    def coef_copy(a, b):
        src, size, dst = halo_part(a, b, 2)
        k = RING1.index((a, b))
        return pltpu.make_async_remote_copy(
            src_ref=coef.at[pl.ds(2 + src[0], size[0]), pl.ds(2 + src[1], size[1])],
            dst_ref=coef.at[pl.ds(dst[0], size[0]), pl.ds(dst[1], size[1])],
            send_sem=coef_send.at[k], recv_sem=coef_recv.at[k], device_id=at(a, b), device_id_type=MESH,
        )

    def col_copy(a, b):
        place = PLACE[-b]
        return pltpu.make_async_remote_copy(
            src_ref=coarse.at[2, 0], dst_ref=coarse.at[2, place],
            send_sem=coarse_send.at[0, place], recv_sem=coarse_recv.at[0, place], device_id=at(a, b), device_id_type=MESH,
        )

    def row_copy(a, b):
        place = PLACE[-a]
        return pltpu.make_async_remote_copy(
            src_ref=coarse.at[2, 0], dst_ref=coarse.at[2 - a, 0],
            send_sem=coarse_send.at[1, place], recv_sem=coarse_recv.at[1, place], device_id=at(a, b), device_id_type=MESH,
        )

    def hand_on(a, b):
        place = PLACE[-a]
        return pltpu.make_async_remote_copy(
            src_ref=coarse.at[2, pl.ds(1, 4)], dst_ref=coarse.at[2 - a, pl.ds(1, 4)],
            send_sem=coarse_send.at[2, place], recv_sem=coarse_recv.at[2, place], device_id=at(a, b), device_id_type=MESH,
        )

    load_vec.wait()
    load_leaf.wait()
    for p in range(LX * LY):
        i, j = p // LY, p % LY
        coef[2 + i, 2 + j] = dot_t(vecs[1 + i, 1 + j], leafb[i, j]).astype(BF16)
    load_cbasis.wait()
    own = jnp.zeros((RHS, COARSE), F32)
    for p in range(LX * LY):
        i, j = p // LY, p % LY
        own += dot(coef[2 + i, 2 + j], cbasis[i, j])
    coarse[2, 0] = own

    above, below = jnp.minimum(row, 2), jnp.minimum(N_ROW - 1 - row, 2)
    ahead, behind = jnp.minimum(col, 2), jnp.minimum(N_COL - 1 - col, 2)
    corners = (jnp.minimum(row, 1) + jnp.minimum(N_ROW - 1 - row, 1)) * (jnp.minimum(col, 1) + jnp.minimum(N_COL - 1 - col, 1))
    pl.semaphore_wait(barrier, above + below + ahead + behind + corners)
    each(COLS, lambda a, b: col_copy(a, b).start())
    each(ROWS, lambda a, b: row_copy(a, b).start())
    each(RING1, lambda a, b: vec_copy(a, b).start())
    each(RING1, lambda a, b: coef_copy(a, b).start())

    for copy in load_small:
        copy.wait()
    for o, (a, b) in enumerate(FAR_OFFSETS):
        ring = [x for x in FAR_OFFSETS if (max(abs(x[0]), abs(x[1])) == 1) == (max(abs(a), abs(b)) == 1)].index((a, b))
        for p in range(LX * LY):
            i, j = p // LY, p % LY
            if max(abs(a), abs(b)) == 1:
                w = 1 - near_mask[i, j, ring]
            else:
                w = far_mask[i, j, ring]
            weights[o, p] = jnp.full((RHS, RANK), w.astype(F32), F32).astype(BF16)

    def near_term(p, s):
        i, j = p // LY, p % LY
        a, b = NEAR_OFFSETS[s]
        lhs = vecs[1 + i + a, 1 + j + b]
        if s != 4:
            live = near_mask[i, j, s if s < 4 else s - 1]
            lhs = lhs * jnp.full((RHS, LEAF), live.astype(F32), F32).astype(BF16)
        return dot(lhs, nblk[p, s])

    def inside(p, s):
        a, b = NEAR_OFFSETS[s]
        return 0 <= p // LY + a < LX and 0 <= p % LY + b < LY

    for p in range(LX * LY):
        if p == NEAR_FIRST:
            each(COLS, lambda a, b: col_copy(-a, -b).wait_recv())
            each(ROWS, lambda a, b: hand_on(a, b).start())
        load_near[p].wait()
        near_acc[p] = sum(near_term(p, s) for s in range(9) if inside(p, s))

    load_ctr.wait()
    for f in range(FAR2):
        whole = ctr[f]
        hi = whole.astype(BF16)
        ctr_hi[f] = hi
        ctr_lo[f] = (whole - hi.astype(F32)).astype(BF16)

    each(RING1, lambda a, b: vec_copy(-a, -b).wait_recv())
    for p in range(LX * LY):
        outer = [s for s in range(9) if not inside(p, s)]
        if outer:
            near_acc[p] += sum(near_term(p, s) for s in outer)

    load_ftr.wait()
    each(RING1, lambda a, b: coef_copy(-a, -b).wait_recv())
    local = jnp.zeros((LX * LY * RHS, RANK), F32)
    for o, (a, b) in enumerate(FAR_OFFSETS):
        lhs = coef[2 + a : 2 + a + LX, 2 + b : 2 + b + LY].reshape(LX * LY, RHS, RANK) * weights[o]
        local += dot(lhs.reshape(LX * LY * RHS, RANK), ftr[o])

    each(ROWS, lambda a, b: row_copy(-a, -b).wait_recv())
    each(ROWS, lambda a, b: hand_on(-a, -b).wait_recv())

    total = jnp.zeros((RHS, COARSE), F32)
    for f in range(FAR2):
        listed = clist[0, f]
        step_b = listed % N_COL - col
        place = jnp.where(step_b == 0, 0, jnp.where(step_b < 0, step_b + 3, step_b + 2))
        whole = coarse[jnp.clip(listed // N_COL - row + 2, 0, 4), jnp.clip(place, 0, 4)]
        hi = whole.astype(BF16)
        lo = (whole - hi.astype(F32)).astype(BF16)
        total += dot(hi, ctr_hi[f]) + (dot(lo, ctr_hi[f]) + dot(hi, ctr_lo[f]))
    coarse_local = total.astype(BF16)
    for p in range(LX * LY):
        i, j = p // LY, p % LY
        down = dot_t(coarse_local, cbasis[i, j])
        both = (local[p * RHS : (p + 1) * RHS] + down).astype(BF16)
        out_ref[i, j] = near_acc[p] + dot(both, leafb[i, j])

    each(RING1, lambda a, b: vec_copy(a, b).wait_send())
    each(RING1, lambda a, b: coef_copy(a, b).wait_send())
    each(COLS, lambda a, b: col_copy(a, b).wait_send())
    each(ROWS, lambda a, b: row_copy(a, b).wait_send())
    each(ROWS, lambda a, b: hand_on(a, b).wait_send())


def per_device(vectors, near_blocks, near_mask, far_mask, leaf_basis, far_transfer, coarse_basis, coarse_list, coarse_transfer):
    any_ = pl.BlockSpec(memory_space=pltpu.HBM)
    vmem = pl.BlockSpec(memory_space=pltpu.VMEM)
    dma = pltpu.SemaphoreType.DMA
    operands = [
        pltpu.with_memory_space_constraint(x, pltpu.HBM)
        for x in (
            vectors, near_blocks, near_mask, far_mask, leaf_basis.swapaxes(2, 3), far_transfer, coarse_basis, coarse_list,
            coarse_transfer[0],
        )
    ]
    return pl.pallas_call(
        kernel,
        out_shape=jax.ShapeDtypeStruct((LX, LY, RHS, LEAF), F32),
        in_specs=[any_] * 9,
        out_specs=vmem,
        scratch_shapes=[
            pltpu.VMEM((LX + 2, LY + 2, RHS, LEAF), BF16),
            pltpu.VMEM((LX + 4, LY + 4, RHS, RANK), BF16),
            pltpu.VMEM((5, 5, RHS, COARSE), F32),
            pltpu.VMEM((LX * LY, 9, LEAF, LEAF), BF16),
            pltpu.VMEM((LX, LY, RANK, LEAF), BF16),
            pltpu.VMEM((24, RANK, RANK), BF16),
            pltpu.VMEM((LX, LY, RANK, COARSE), BF16),
            pltpu.VMEM((FAR2, COARSE, COARSE), F32),
            pltpu.VMEM((FAR2, COARSE, COARSE), BF16),
            pltpu.VMEM((FAR2, COARSE, COARSE), BF16),
            pltpu.VMEM((LX * LY, RHS, LEAF), F32),
            pltpu.VMEM((24, LX * LY, RHS, RANK), BF16),
            pltpu.SMEM((LX, LY, 8), jnp.int32),
            pltpu.SMEM((LX, LY, 16), jnp.int32),
            pltpu.SMEM((1, FAR2), jnp.int32),
            dma((LX * LY,)),
            dma((8,)),
            dma((8,)),
            dma((8,)),
            dma((8,)),
            dma((8,)),
            dma((3, 5)),
            dma((3, 5)),
        ],
        compiler_params=pltpu.CompilerParams(
            collective_id=0, has_side_effects=True, vmem_limit_bytes=40 * 1024 * 1024
        ),
    )(*operands)


def solution(mesh):
    placed = (
        P("row", "col", None, None),
        P("row", "col", None, None, None),
        P("row", "col", None),
        P("row", "col", None),
        P("row", "col", None, None),
        P(),
        P("row", "col", None, None),
        P(("row", "col"), None),
        P(("row", "col"), None, None, None),
    )
    return jax.shard_map(
        per_device, mesh=mesh, in_specs=placed, out_specs=P("row", "col", None, None), check_vma=False
    )
```

```python
import functools

import jax
import jax.numpy as jnp
from jax import lax
from jax.experimental import pallas as pl
from jax.experimental.pallas import tpu as pltpu
from jax.sharding import PartitionSpec as P

MESH = pl.DeviceIdType.MESH
LX, LY, RHS, LEAF, RANK, COARSE, FAR2 = 4, 2, 16, 256, 64, 256, 8
N_ROW, N_COL = 8, 16
NEAR_OFFSETS = [(a, b) for a in (-1, 0, 1) for b in (-1, 0, 1)]
FAR_OFFSETS = [(a, b) for a in range(-2, 3) for b in range(-2, 3) if (a, b) != (0, 0)]
RING1 = [(a, b) for a, b in NEAR_OFFSETS if (a, b) != (0, 0)]
COLS = [(0, -2), (0, 2), (0, -1), (0, 1)]
ROWS = [(-2, 0), (2, 0), (-1, 0), (1, 0)]
CORNERS = [(-1, -1), (-1, 1), (1, -1), (1, 1)]
PARTNERS = COLS + ROWS + CORNERS
NEAR_FIRST = 6
PLACE = {0: 0, -2: 1, -1: 2, 1: 3, 2: 4}
BF16, F32 = jnp.bfloat16, jnp.float32


def dot(lhs, rhs):
    return lax.dot_general(lhs, rhs, (((1,), (0,)), ((), ())), preferred_element_type=F32)


def dot_t(lhs, rhs):
    return lax.dot_general(lhs, rhs, (((1,), (1,)), ((), ())), preferred_element_type=F32)


def halo_part(a, b, width):
    src, size, dst = [], [], []
    for step, own in ((a, LX), (b, LY)):
        size.append(own if step == 0 else width)
        src.append(own - width if step == 1 else 0)
        dst.append({-1: width + own, 0: width, 1: 0}[step])
    return src, size, dst


def kernel(
    vec_hbm, near_hbm, near_mask_hbm, far_mask_hbm, leaf_hbm, transfer_hbm, cbasis_hbm, clist_hbm, ctrans_hbm,
    out_ref,
    vecs, coef, coarse, nblk, leafb, ftr, cbasis, ctr, ctr_hi, ctr_lo, near_acc, weights,
    near_mask, far_mask, clist,
    near_sem, load_sem, vec_send, vec_recv, coef_send, coef_recv, coarse_send, coarse_recv,
):
    row = lax.axis_index("row")
    col = lax.axis_index("col")

    def at(a, b):
        return (row + a, col + b)

    there = {}
    for a, b in PARTNERS:
        r, c = at(a, b)
        there[a, b] = (r >= 0) & (r < N_ROW) & (c >= 0) & (c < N_COL)

    def each(offsets, step):
        for a, b in offsets:
            pl.when(there[a, b])(functools.partial(step, a, b))

    barrier = pltpu.get_barrier_semaphore()
    each(PARTNERS, lambda a, b: pl.semaphore_signal(barrier, inc=1, device_id=at(a, b), device_id_type=MESH))

    load_vec = pltpu.make_async_copy(vec_hbm, vecs.at[pl.ds(1, LX), pl.ds(1, LY)], load_sem.at[2])
    load_vec.start()
    load_leaf = pltpu.make_async_copy(leaf_hbm, leafb, load_sem.at[0])
    load_leaf.start()
    load_cbasis = pltpu.make_async_copy(cbasis_hbm, cbasis, load_sem.at[1])
    load_cbasis.start()

    load_small = []
    for k, (src, dst) in enumerate(((near_mask_hbm, near_mask), (far_mask_hbm, far_mask), (clist_hbm, clist))):
        load_small.append(pltpu.make_async_copy(src, dst, load_sem.at[5 + k]))
        load_small[-1].start()
    load_ctr = pltpu.make_async_copy(ctrans_hbm, ctr, load_sem.at[3])
    load_near = []
    for p in range(LX * LY):
        load_near.append(pltpu.make_async_copy(near_hbm.at[p // LY, p % LY], nblk.at[p], near_sem.at[p]))
        load_near[-1].start()
        if p == 0:
            load_ctr.start()
    load_ftr = pltpu.make_async_copy(transfer_hbm, ftr, load_sem.at[4])
    load_ftr.start()

    for ref, width, last in ((vecs, 1, LEAF), (coef, 2, RANK)):
        edge = (width, LY + 2 * width, RHS, last)
        side = (LX + 2 * width, width, RHS, last)
        for missing, place, shape in (
            (row == 0, (pl.ds(0, width),), edge),
            (row == N_ROW - 1, (pl.ds(width + LX, width),), edge),
            (col == 0, (slice(None), pl.ds(0, width)), side),
            (col == N_COL - 1, (slice(None), pl.ds(width + LY, width)), side),
        ):
            @pl.when(missing)
            def _():
                ref[place] = jnp.zeros(shape, BF16)
    for a, b in COLS:
        @pl.when(jnp.logical_not(there[a, b]))
        def _():
            coarse[2, PLACE[b]] = jnp.zeros((RHS, COARSE), F32)

    def vec_copy(a, b):
        src, size, dst = halo_part(a, b, 1)
        k = RING1.index((a, b))
        return pltpu.make_async_remote_copy(
            src_ref=vecs.at[pl.ds(1 + src[0], size[0]), pl.ds(1 + src[1], size[1])],
            dst_ref=vecs.at[pl.ds(dst[0], size[0]), pl.ds(dst[1], size[1])],
            send_sem=vec_send.at[k], recv_sem=vec_recv.at[k], device_id=at(a, b), device_id_type=MESH,
        )

    def coef_copy(a, b):
        src, size, dst = halo_part(a, b, 2)
        k = RING1.index((a, b))
        return pltpu.make_async_remote_copy(
            src_ref=coef.at[pl.ds(2 + src[0], size[0]), pl.ds(2 + src[1], size[1])],
            dst_ref=coef.at[pl.ds(dst[0], size[0]), pl.ds(dst[1], size[1])],
            send_sem=coef_send.at[k], recv_sem=coef_recv.at[k], device_id=at(a, b), device_id_type=MESH,
        )

    def col_copy(a, b):
        place = PLACE[-b]
        return pltpu.make_async_remote_copy(
            src_ref=coarse.at[2, 0], dst_ref=coarse.at[2, place],
            send_sem=coarse_send.at[0, place], recv_sem=coarse_recv.at[0, place], device_id=at(a, b), device_id_type=MESH,
        )

    def row_copy(a, b):
        place = PLACE[-a]
        return pltpu.make_async_remote_copy(
            src_ref=coarse.at[2, 0], dst_ref=coarse.at[2 - a, 0],
            send_sem=coarse_send.at[1, place], recv_sem=coarse_recv.at[1, place], device_id=at(a, b), device_id_type=MESH,
        )

    def hand_on(a, b):
        place = PLACE[-a]
        return pltpu.make_async_remote_copy(
            src_ref=coarse.at[2, pl.ds(1, 4)], dst_ref=coarse.at[2 - a, pl.ds(1, 4)],
            send_sem=coarse_send.at[2, place], recv_sem=coarse_recv.at[2, place], device_id=at(a, b), device_id_type=MESH,
        )

    load_vec.wait()
    load_leaf.wait()
    leaf = [(p // LY, p % LY) for p in range(LX * LY)]
    coeffs = [dot_t(vecs[1 + i, 1 + j], leafb[i, j]).astype(BF16) for i, j in leaf]
    for (i, j), value in zip(leaf, coeffs):
        coef[2 + i, 2 + j] = value
    load_cbasis.wait()
    own = sum(dot(value, cbasis[i, j]) for (i, j), value in zip(leaf, coeffs))
    coarse[2, 0] = own

    above, below = jnp.minimum(row, 2), jnp.minimum(N_ROW - 1 - row, 2)
    ahead, behind = jnp.minimum(col, 2), jnp.minimum(N_COL - 1 - col, 2)
    corners = (jnp.minimum(row, 1) + jnp.minimum(N_ROW - 1 - row, 1)) * (jnp.minimum(col, 1) + jnp.minimum(N_COL - 1 - col, 1))
    pl.semaphore_wait(barrier, above + below + ahead + behind + corners)
    each(COLS, lambda a, b: col_copy(a, b).start())
    each(ROWS, lambda a, b: row_copy(a, b).start())
    each(RING1, lambda a, b: vec_copy(a, b).start())
    each(RING1, lambda a, b: coef_copy(a, b).start())

    for copy in load_small:
        copy.wait()
    for o, (a, b) in enumerate(FAR_OFFSETS):
        ring = [x for x in FAR_OFFSETS if (max(abs(x[0]), abs(x[1])) == 1) == (max(abs(a), abs(b)) == 1)].index((a, b))
        for p in range(LX * LY):
            i, j = p // LY, p % LY
            if max(abs(a), abs(b)) == 1:
                w = 1 - near_mask[i, j, ring]
            else:
                w = far_mask[i, j, ring]
            weights[o, p] = jnp.full((RHS, RANK), w.astype(F32), F32).astype(BF16)

    def near_term(p, s):
        i, j = p // LY, p % LY
        a, b = NEAR_OFFSETS[s]
        lhs = vecs[1 + i + a, 1 + j + b]
        if s != 4:
            live = near_mask[i, j, s if s < 4 else s - 1]
            lhs = lhs * jnp.full((RHS, LEAF), live.astype(F32), F32).astype(BF16)
        return dot(lhs, nblk[p, s])

    def inside(p, s):
        a, b = NEAR_OFFSETS[s]
        return 0 <= p // LY + a < LX and 0 <= p % LY + b < LY

    for p in range(LX * LY):
        if p == NEAR_FIRST:
            each(COLS, lambda a, b: col_copy(-a, -b).wait_recv())
            each(ROWS, lambda a, b: hand_on(a, b).start())
        load_near[p].wait()
        near_acc[p] = sum(near_term(p, s) for s in range(9) if inside(p, s))

    load_ctr.wait()
    for f in range(FAR2):
        whole = ctr[f]
        hi = whole.astype(BF16)
        ctr_hi[f] = hi
        ctr_lo[f] = (whole - hi.astype(F32)).astype(BF16)

    each(RING1, lambda a, b: vec_copy(-a, -b).wait_recv())
    for p in range(LX * LY):
        outer = [s for s in range(9) if not inside(p, s)]
        if outer:
            near_acc[p] += sum(near_term(p, s) for s in outer)

    load_ftr.wait()
    each(RING1, lambda a, b: coef_copy(-a, -b).wait_recv())
    local = jnp.zeros((LX * LY * RHS, RANK), F32)
    for o, (a, b) in enumerate(FAR_OFFSETS):
        lhs = coef[2 + a : 2 + a + LX, 2 + b : 2 + b + LY].reshape(LX * LY, RHS, RANK) * weights[o]
        local += dot(lhs.reshape(LX * LY * RHS, RANK), ftr[o])

    each(ROWS, lambda a, b: row_copy(-a, -b).wait_recv())
    each(ROWS, lambda a, b: hand_on(-a, -b).wait_recv())

    total = jnp.zeros((RHS, COARSE), F32)
    both = jnp.zeros((2 * RHS, COARSE), F32)
    for f in range(FAR2):
        listed = clist[0, f]
        step_b = listed % N_COL - col
        place = jnp.where(step_b == 0, 0, jnp.where(step_b < 0, step_b + 3, step_b + 2))
        whole = coarse[jnp.clip(listed // N_COL - row + 2, 0, 4), jnp.clip(place, 0, 4)]
        hi = whole.astype(BF16)
        lo = (whole - hi.astype(F32)).astype(BF16)
        both += dot(jnp.concatenate([hi, lo], axis=0), ctr_hi[f])
        total += dot(hi, ctr_lo[f])
    total = both[:RHS] + (both[RHS:] + total)
    coarse_local = total.astype(BF16)
    down = [dot_t(coarse_local, cbasis[p // LY, p % LY]) for p in range(LX * LY)]
    whole = [(local[p * RHS : (p + 1) * RHS] + down[p]).astype(BF16) for p in range(LX * LY)]
    far = [dot(whole[p], leafb[p // LY, p % LY]) for p in range(LX * LY)]
    applied = [near_acc[p] + far[p] for p in range(LX * LY)]
    for p in range(LX * LY):
        out_ref[p // LY, p % LY] = applied[p]

    each(RING1, lambda a, b: vec_copy(a, b).wait_send())
    each(RING1, lambda a, b: coef_copy(a, b).wait_send())
    each(COLS, lambda a, b: col_copy(a, b).wait_send())
    each(ROWS, lambda a, b: row_copy(a, b).wait_send())
    each(ROWS, lambda a, b: hand_on(a, b).wait_send())


def per_device(vectors, near_blocks, near_mask, far_mask, leaf_basis, far_transfer, coarse_basis, coarse_list, coarse_transfer):
    any_ = pl.BlockSpec(memory_space=pltpu.HBM)
    vmem = pl.BlockSpec(memory_space=pltpu.VMEM)
    dma = pltpu.SemaphoreType.DMA
    operands = [
        pltpu.with_memory_space_constraint(x, pltpu.HBM)
        for x in (
            vectors, near_blocks, near_mask, far_mask, leaf_basis.swapaxes(2, 3), far_transfer, coarse_basis, coarse_list,
            coarse_transfer[0],
        )
    ]
    return pl.pallas_call(
        kernel,
        out_shape=jax.ShapeDtypeStruct((LX, LY, RHS, LEAF), F32),
        in_specs=[any_] * 9,
        out_specs=vmem,
        scratch_shapes=[
            pltpu.VMEM((LX + 2, LY + 2, RHS, LEAF), BF16),
            pltpu.VMEM((LX + 4, LY + 4, RHS, RANK), BF16),
            pltpu.VMEM((5, 5, RHS, COARSE), F32),
            pltpu.VMEM((LX * LY, 9, LEAF, LEAF), BF16),
            pltpu.VMEM((LX, LY, RANK, LEAF), BF16),
            pltpu.VMEM((24, RANK, RANK), BF16),
            pltpu.VMEM((LX, LY, RANK, COARSE), BF16),
            pltpu.VMEM((FAR2, COARSE, COARSE), F32),
            pltpu.VMEM((FAR2, COARSE, COARSE), BF16),
            pltpu.VMEM((FAR2, COARSE, COARSE), BF16),
            pltpu.VMEM((LX * LY, RHS, LEAF), F32),
            pltpu.VMEM((24, LX * LY, RHS, RANK), BF16),
            pltpu.SMEM((LX, LY, 8), jnp.int32),
            pltpu.SMEM((LX, LY, 16), jnp.int32),
            pltpu.SMEM((1, FAR2), jnp.int32),
            dma((LX * LY,)),
            dma((8,)),
            dma((8,)),
            dma((8,)),
            dma((8,)),
            dma((8,)),
            dma((3, 5)),
            dma((3, 5)),
        ],
        compiler_params=pltpu.CompilerParams(
            collective_id=0, has_side_effects=True, vmem_limit_bytes=40 * 1024 * 1024
        ),
    )(*operands)


def solution(mesh):
    placed = (
        P("row", "col", None, None),
        P("row", "col", None, None, None),
        P("row", "col", None),
        P("row", "col", None),
        P("row", "col", None, None),
        P(),
        P("row", "col", None, None),
        P(("row", "col"), None),
        P(("row", "col"), None, None, None),
    )
    return jax.shard_map(
        per_device, mesh=mesh, in_specs=placed, out_specs=P("row", "col", None, None), check_vma=False
    )
```

```python
import functools

import jax
import jax.numpy as jnp
from jax import lax
from jax.experimental import pallas as pl
from jax.experimental.pallas import tpu as pltpu
from jax.sharding import PartitionSpec as P

MESH = pl.DeviceIdType.MESH
LX, LY, RHS, LEAF, RANK, COARSE, FAR2 = 4, 2, 16, 256, 64, 256, 8
N_ROW, N_COL = 8, 16
NEAR_OFFSETS = [(a, b) for a in (-1, 0, 1) for b in (-1, 0, 1)]
FAR_OFFSETS = [(a, b) for a in range(-2, 3) for b in range(-2, 3) if (a, b) != (0, 0)]
RING1 = [(a, b) for a, b in NEAR_OFFSETS if (a, b) != (0, 0)]
COLS = [(0, -2), (0, 2), (0, -1), (0, 1)]
ROWS = [(-2, 0), (2, 0), (-1, 0), (1, 0)]
CORNERS = [(-1, -1), (-1, 1), (1, -1), (1, 1)]
PARTNERS = COLS + ROWS + CORNERS
NEAR_FIRST = 6
PLACE = {0: 0, -2: 1, -1: 2, 1: 3, 2: 4}
BF16, F32, I16, I32 = jnp.bfloat16, jnp.float32, jnp.int16, jnp.int32
MESSAGE = COARSE + 128
LEAST = 2.0**-100


def dot(lhs, rhs):
    return lax.dot_general(lhs, rhs, (((1,), (0,)), ((), ())), preferred_element_type=F32)


def dot_t(lhs, rhs):
    return lax.dot_general(lhs, rhs, (((1,), (1,)), ((), ())), preferred_element_type=F32)


def halo_part(a, b, width):
    src, size, dst = [], [], []
    for step, own in ((a, LX), (b, LY)):
        size.append(own if step == 0 else width)
        src.append(own - width if step == 1 else 0)
        dst.append({-1: width + own, 0: width, 1: 0}[step])
    return src, size, dst


def encoded(values):
    largest = jnp.max(jnp.abs(values), axis=1, keepdims=True)
    exponent = jnp.floor(jnp.log2(jnp.maximum(largest, LEAST))) + 1.0
    whole = jnp.clip(jnp.round(values * jnp.exp2(15.0 - exponent)), -32767.0, 32767.0)
    tail = jnp.broadcast_to(exponent, (RHS, MESSAGE - COARSE))
    return jnp.concatenate([whole, tail], axis=1).astype(I32).astype(I16)


def decoded(message):
    numbers = message.astype(I32).astype(F32)
    scale = jnp.exp2(numbers[:, COARSE:] - 15.0)
    return numbers[:, :COARSE] * jnp.concatenate([scale] * (COARSE // scale.shape[1]), axis=1)


def kernel(
    vec_hbm, near_hbm, near_mask_hbm, far_mask_hbm, leaf_hbm, transfer_hbm, cbasis_hbm, clist_hbm, ctrans_hbm,
    out_ref,
    vecs, coef, coarse, nblk, leafb, ftr, cbasis, ctr, ctr_hi, ctr_lo, near_acc, weights,
    near_mask, far_mask, clist,
    near_sem, load_sem, vec_send, vec_recv, coef_send, coef_recv, coarse_send, coarse_recv,
):
    row = lax.axis_index("row")
    col = lax.axis_index("col")

    def at(a, b):
        return (row + a, col + b)

    there = {}
    for a, b in PARTNERS:
        r, c = at(a, b)
        there[a, b] = (r >= 0) & (r < N_ROW) & (c >= 0) & (c < N_COL)

    def each(offsets, step):
        for a, b in offsets:
            pl.when(there[a, b])(functools.partial(step, a, b))

    barrier = pltpu.get_barrier_semaphore()
    each(PARTNERS, lambda a, b: pl.semaphore_signal(barrier, inc=1, device_id=at(a, b), device_id_type=MESH))

    load_vec = pltpu.make_async_copy(vec_hbm, vecs.at[pl.ds(1, LX), pl.ds(1, LY)], load_sem.at[2])
    load_vec.start()
    load_leaf = pltpu.make_async_copy(leaf_hbm, leafb, load_sem.at[0])
    load_leaf.start()
    load_cbasis = pltpu.make_async_copy(cbasis_hbm, cbasis, load_sem.at[1])
    load_cbasis.start()

    load_small = []
    for k, (src, dst) in enumerate(((near_mask_hbm, near_mask), (far_mask_hbm, far_mask), (clist_hbm, clist))):
        load_small.append(pltpu.make_async_copy(src, dst, load_sem.at[5 + k]))
        load_small[-1].start()
    load_ctr = pltpu.make_async_copy(ctrans_hbm, ctr, load_sem.at[3])
    load_near = []
    for p in range(LX * LY):
        load_near.append(pltpu.make_async_copy(near_hbm.at[p // LY, p % LY], nblk.at[p], near_sem.at[p]))
        load_near[-1].start()
        if p == 0:
            load_ctr.start()
    load_ftr = pltpu.make_async_copy(transfer_hbm, ftr, load_sem.at[4])
    load_ftr.start()

    for ref, width, last in ((vecs, 1, LEAF), (coef, 2, RANK)):
        edge = (width, LY + 2 * width, RHS, last)
        side = (LX + 2 * width, width, RHS, last)
        for missing, place, shape in (
            (row == 0, (pl.ds(0, width),), edge),
            (row == N_ROW - 1, (pl.ds(width + LX, width),), edge),
            (col == 0, (slice(None), pl.ds(0, width)), side),
            (col == N_COL - 1, (slice(None), pl.ds(width + LY, width)), side),
        ):
            @pl.when(missing)
            def _():
                ref[place] = jnp.zeros(shape, BF16)
    for a, b in COLS:
        @pl.when(jnp.logical_not(there[a, b]))
        def _():
            coarse[2, PLACE[b]] = jnp.zeros((RHS, MESSAGE), I16)

    def vec_copy(a, b):
        src, size, dst = halo_part(a, b, 1)
        k = RING1.index((a, b))
        return pltpu.make_async_remote_copy(
            src_ref=vecs.at[pl.ds(1 + src[0], size[0]), pl.ds(1 + src[1], size[1])],
            dst_ref=vecs.at[pl.ds(dst[0], size[0]), pl.ds(dst[1], size[1])],
            send_sem=vec_send.at[k], recv_sem=vec_recv.at[k], device_id=at(a, b), device_id_type=MESH,
        )

    def coef_copy(a, b):
        src, size, dst = halo_part(a, b, 2)
        k = RING1.index((a, b))
        return pltpu.make_async_remote_copy(
            src_ref=coef.at[pl.ds(2 + src[0], size[0]), pl.ds(2 + src[1], size[1])],
            dst_ref=coef.at[pl.ds(dst[0], size[0]), pl.ds(dst[1], size[1])],
            send_sem=coef_send.at[k], recv_sem=coef_recv.at[k], device_id=at(a, b), device_id_type=MESH,
        )

    def col_copy(a, b):
        place = PLACE[-b]
        return pltpu.make_async_remote_copy(
            src_ref=coarse.at[2, 0], dst_ref=coarse.at[2, place],
            send_sem=coarse_send.at[0, place], recv_sem=coarse_recv.at[0, place], device_id=at(a, b), device_id_type=MESH,
        )

    def row_copy(a, b):
        place = PLACE[-a]
        return pltpu.make_async_remote_copy(
            src_ref=coarse.at[2, 0], dst_ref=coarse.at[2 - a, 0],
            send_sem=coarse_send.at[1, place], recv_sem=coarse_recv.at[1, place], device_id=at(a, b), device_id_type=MESH,
        )

    def hand_on(side, a, b):
        place = PLACE[-a]
        pair = pl.ds(1 + 2 * side, 2)
        return pltpu.make_async_remote_copy(
            src_ref=coarse.at[2, pair], dst_ref=coarse.at[2 - a, pair],
            send_sem=coarse_send.at[2 + side, place], recv_sem=coarse_recv.at[2 + side, place],
            device_id=at(a, b), device_id_type=MESH,
        )

    has_side = (col > 0, col < N_COL - 1)

    def each_side(side, step):
        for a, b in ROWS:
            pl.when(there[a, b] & has_side[side])(functools.partial(step, side, a, b))

    load_vec.wait()
    load_leaf.wait()
    leaf = [(p // LY, p % LY) for p in range(LX * LY)]
    coeffs = [dot_t(vecs[1 + i, 1 + j], leafb[i, j]).astype(BF16) for i, j in leaf]
    for (i, j), value in zip(leaf, coeffs):
        coef[2 + i, 2 + j] = value
    load_cbasis.wait()
    own = sum(dot(value, cbasis[i, j]) for (i, j), value in zip(leaf, coeffs))
    coarse[2, 0] = encoded(own)

    above, below = jnp.minimum(row, 2), jnp.minimum(N_ROW - 1 - row, 2)
    ahead, behind = jnp.minimum(col, 2), jnp.minimum(N_COL - 1 - col, 2)
    corners = (jnp.minimum(row, 1) + jnp.minimum(N_ROW - 1 - row, 1)) * (jnp.minimum(col, 1) + jnp.minimum(N_COL - 1 - col, 1))
    pl.semaphore_wait(barrier, above + below + ahead + behind + corners)
    each(COLS, lambda a, b: col_copy(a, b).start())
    each(ROWS, lambda a, b: row_copy(a, b).start())
    each(RING1, lambda a, b: vec_copy(a, b).start())
    each(RING1, lambda a, b: coef_copy(a, b).start())

    for copy in load_small:
        copy.wait()
    for o, (a, b) in enumerate(FAR_OFFSETS):
        ring = [x for x in FAR_OFFSETS if (max(abs(x[0]), abs(x[1])) == 1) == (max(abs(a), abs(b)) == 1)].index((a, b))
        for p in range(LX * LY):
            i, j = p // LY, p % LY
            if max(abs(a), abs(b)) == 1:
                w = 1 - near_mask[i, j, ring]
            else:
                w = far_mask[i, j, ring]
            weights[o, p] = jnp.full((RHS, RANK), w.astype(F32), F32).astype(BF16)

    def near_term(p, s):
        i, j = p // LY, p % LY
        a, b = NEAR_OFFSETS[s]
        lhs = vecs[1 + i + a, 1 + j + b]
        if s != 4:
            live = near_mask[i, j, s if s < 4 else s - 1]
            lhs = lhs * jnp.full((RHS, LEAF), live.astype(F32), F32).astype(BF16)
        return dot(lhs, nblk[p, s])

    def inside(p, s):
        a, b = NEAR_OFFSETS[s]
        return 0 <= p // LY + a < LX and 0 <= p % LY + b < LY

    for p in range(LX * LY):
        if p == NEAR_FIRST:
            for side in (0, 1):
                each([k for k in COLS if (k[1] > 0) == side], lambda a, b: col_copy(-a, -b).wait_recv())
                each_side(side, lambda side, a, b: hand_on(side, a, b).start())
        load_near[p].wait()
        near_acc[p] = sum(near_term(p, s) for s in range(9) if inside(p, s))

    load_ctr.wait()
    for f in range(FAR2):
        whole = ctr[f]
        hi = whole.astype(BF16)
        ctr_hi[f] = hi
        ctr_lo[f] = (whole - hi.astype(F32)).astype(BF16)

    each(RING1, lambda a, b: vec_copy(-a, -b).wait_recv())
    for p in range(LX * LY):
        outer = [s for s in range(9) if not inside(p, s)]
        if outer:
            near_acc[p] += sum(near_term(p, s) for s in outer)

    load_ftr.wait()
    each(RING1, lambda a, b: coef_copy(-a, -b).wait_recv())
    local = jnp.zeros((LX * LY * RHS, RANK), F32)
    for o, (a, b) in enumerate(FAR_OFFSETS):
        lhs = coef[2 + a : 2 + a + LX, 2 + b : 2 + b + LY].reshape(LX * LY, RHS, RANK) * weights[o]
        local += dot(lhs.reshape(LX * LY * RHS, RANK), ftr[o])

    each(RING1, lambda a, b: vec_copy(a, b).wait_send())
    each(RING1, lambda a, b: coef_copy(a, b).wait_send())
    each(COLS, lambda a, b: col_copy(a, b).wait_send())
    each(ROWS, lambda a, b: row_copy(a, b).wait_send())
    each(ROWS, lambda a, b: row_copy(-a, -b).wait_recv())
    for side in (0, 1):
        each_side(side, lambda side, a, b: hand_on(side, -a, -b).wait_recv())

    total = jnp.zeros((RHS, COARSE), F32)
    both = jnp.zeros((2 * RHS, COARSE), F32)
    for f in range(FAR2):
        listed = clist[0, f]
        step_b = listed % N_COL - col
        place = jnp.where(step_b == 0, 0, jnp.where(step_b < 0, step_b + 3, step_b + 2))
        whole = decoded(coarse[jnp.clip(listed // N_COL - row + 2, 0, 4), jnp.clip(place, 0, 4)])
        hi = whole.astype(BF16)
        lo = (whole - hi.astype(F32)).astype(BF16)
        both += dot(jnp.concatenate([hi, lo], axis=0), ctr_hi[f])
        total += dot(hi, ctr_lo[f])
    total = both[:RHS] + (both[RHS:] + total)
    coarse_local = total.astype(BF16)
    down = [dot_t(coarse_local, cbasis[p // LY, p % LY]) for p in range(LX * LY)]
    whole = [(local[p * RHS : (p + 1) * RHS] + down[p]).astype(BF16) for p in range(LX * LY)]
    far = [dot(whole[p], leafb[p // LY, p % LY]) for p in range(LX * LY)]
    applied = [near_acc[p] + far[p] for p in range(LX * LY)]
    for p in range(LX * LY):
        out_ref[p // LY, p % LY] = applied[p]

    for side in (0, 1):
        each_side(side, lambda side, a, b: hand_on(side, a, b).wait_send())


def per_device(vectors, near_blocks, near_mask, far_mask, leaf_basis, far_transfer, coarse_basis, coarse_list, coarse_transfer):
    any_ = pl.BlockSpec(memory_space=pltpu.HBM)
    vmem = pl.BlockSpec(memory_space=pltpu.VMEM)
    dma = pltpu.SemaphoreType.DMA
    operands = [
        pltpu.with_memory_space_constraint(x, pltpu.HBM)
        for x in (
            vectors, near_blocks, near_mask, far_mask, leaf_basis.swapaxes(2, 3), far_transfer, coarse_basis, coarse_list,
            coarse_transfer[0],
        )
    ]
    return pl.pallas_call(
        kernel,
        out_shape=jax.ShapeDtypeStruct((LX, LY, RHS, LEAF), F32),
        in_specs=[any_] * 9,
        out_specs=vmem,
        scratch_shapes=[
            pltpu.VMEM((LX + 2, LY + 2, RHS, LEAF), BF16),
            pltpu.VMEM((LX + 4, LY + 4, RHS, RANK), BF16),
            pltpu.VMEM((5, 5, RHS, MESSAGE), I16),
            pltpu.VMEM((LX * LY, 9, LEAF, LEAF), BF16),
            pltpu.VMEM((LX, LY, RANK, LEAF), BF16),
            pltpu.VMEM((24, RANK, RANK), BF16),
            pltpu.VMEM((LX, LY, RANK, COARSE), BF16),
            pltpu.VMEM((FAR2, COARSE, COARSE), F32),
            pltpu.VMEM((FAR2, COARSE, COARSE), BF16),
            pltpu.VMEM((FAR2, COARSE, COARSE), BF16),
            pltpu.VMEM((LX * LY, RHS, LEAF), F32),
            pltpu.VMEM((24, LX * LY, RHS, RANK), BF16),
            pltpu.SMEM((LX, LY, 8), jnp.int32),
            pltpu.SMEM((LX, LY, 16), jnp.int32),
            pltpu.SMEM((1, FAR2), jnp.int32),
            dma((LX * LY,)),
            dma((8,)),
            dma((8,)),
            dma((8,)),
            dma((8,)),
            dma((8,)),
            dma((4, 5)),
            dma((4, 5)),
        ],
        compiler_params=pltpu.CompilerParams(
            collective_id=0, has_side_effects=True, vmem_limit_bytes=40 * 1024 * 1024
        ),
    )(*operands)


def solution(mesh):
    placed = (
        P("row", "col", None, None),
        P("row", "col", None, None, None),
        P("row", "col", None),
        P("row", "col", None),
        P("row", "col", None, None),
        P(),
        P("row", "col", None, None),
        P(("row", "col"), None),
        P(("row", "col"), None, None, None),
    )
    return jax.shard_map(
        per_device, mesh=mesh, in_specs=placed, out_specs=P("row", "col", None, None), check_vma=False
    )
```

```python
import functools

import jax
import jax.numpy as jnp
from jax import lax
from jax.experimental import pallas as pl
from jax.experimental.pallas import tpu as pltpu
from jax.sharding import PartitionSpec as P

MESH = pl.DeviceIdType.MESH
LX, LY, RHS, LEAF, RANK, COARSE, FAR2 = 4, 2, 16, 256, 64, 256, 8
N_ROW, N_COL = 8, 16
NEAR_OFFSETS = [(a, b) for a in (-1, 0, 1) for b in (-1, 0, 1)]
FAR_OFFSETS = [(a, b) for a in range(-2, 3) for b in range(-2, 3) if (a, b) != (0, 0)]
RING1 = [(a, b) for a, b in NEAR_OFFSETS if (a, b) != (0, 0)]
COLS = [(0, -2), (0, 2), (0, -1), (0, 1)]
ROWS = [(-2, 0), (2, 0), (-1, 0), (1, 0)]
CORNERS = [(-1, -1), (-1, 1), (1, -1), (1, 1)]
PARTNERS = COLS + ROWS
SIDES = [(-1, 0), (1, 0), (0, -1), (0, 1)]
NEAR_FIRST = 3
PLACE = {0: 0, -2: 1, -1: 2, 1: 3, 2: 4}
BF16, F32, I16, I32 = jnp.bfloat16, jnp.float32, jnp.int16, jnp.int32
MESSAGE = COARSE + 128
LEAST = 2.0**-100


def dot(lhs, rhs):
    return lax.dot_general(lhs, rhs, (((1,), (0,)), ((), ())), preferred_element_type=F32)


def dot_t(lhs, rhs):
    return lax.dot_general(lhs, rhs, (((1,), (1,)), ((), ())), preferred_element_type=F32)


def halo_part(a, b, width):
    src, size, dst = [], [], []
    for step, own in ((a, LX), (b, LY)):
        size.append(own if step == 0 else width)
        src.append(own - width if step == 1 else 0)
        dst.append({-1: width + own, 0: width, 1: 0}[step])
    return src, size, dst


def encoded(values):
    largest = jnp.max(jnp.abs(values), axis=1, keepdims=True)
    exponent = jnp.floor(jnp.log2(jnp.maximum(largest, LEAST))) + 1.0
    whole = jnp.clip(jnp.round(values * jnp.exp2(15.0 - exponent)), -32767.0, 32767.0)
    tail = jnp.broadcast_to(exponent, (RHS, MESSAGE - COARSE))
    return jnp.concatenate([whole, tail], axis=1).astype(I32).astype(I16)


def decoded(message):
    numbers = message.astype(I32).astype(F32)
    scale = jnp.exp2(numbers[:, COARSE:] - 15.0)
    return numbers[:, :COARSE] * jnp.concatenate([scale] * (COARSE // scale.shape[1]), axis=1)


def kernel(
    vec_hbm, near_hbm, near_mask_hbm, far_mask_hbm, leaf_hbm, transfer_hbm, cbasis_hbm, clist_hbm, ctrans_hbm,
    out_ref,
    vecs, coef, coarse, nblk, leafb, ftr, cbasis, ctr, ctr_hi, ctr_lo, near_acc, weights,
    near_mask, far_mask, clist,
    near_sem, load_sem, vec_send, vec_recv, coef_send, coef_recv, coarse_send, coarse_recv, ready,
):
    row = lax.axis_index("row")
    col = lax.axis_index("col")

    def at(a, b):
        return (row + a, col + b)

    there = {}
    for a, b in PARTNERS + CORNERS:
        r, c = at(a, b)
        there[a, b] = (r >= 0) & (r < N_ROW) & (c >= 0) & (c < N_COL)

    def each(offsets, step):
        for a, b in offsets:
            pl.when(there[a, b])(functools.partial(step, a, b))

    barrier = pltpu.get_barrier_semaphore()
    each(PARTNERS, lambda a, b: pl.semaphore_signal(barrier, inc=1, device_id=at(a, b), device_id_type=MESH))

    load_vec = pltpu.make_async_copy(vec_hbm, vecs.at[pl.ds(1, LX), pl.ds(1, LY)], load_sem.at[2])
    load_vec.start()
    load_leaf = pltpu.make_async_copy(leaf_hbm, leafb, load_sem.at[0])
    load_leaf.start()
    load_cbasis = pltpu.make_async_copy(cbasis_hbm, cbasis, load_sem.at[1])
    load_cbasis.start()

    load_small = []
    for k, (src, dst) in enumerate(((near_mask_hbm, near_mask), (far_mask_hbm, far_mask), (clist_hbm, clist))):
        load_small.append(pltpu.make_async_copy(src, dst, load_sem.at[5 + k]))
        load_small[-1].start()
    for ref, width, last in ((vecs, 1, LEAF), (coef, 2, RANK)):
        edge = (width, LY + 2 * width, RHS, last)
        side = (LX + 2 * width, width, RHS, last)
        for missing, place, shape in (
            (row == 0, (pl.ds(0, width),), edge),
            (row == N_ROW - 1, (pl.ds(width + LX, width),), edge),
            (col == 0, (slice(None), pl.ds(0, width)), side),
            (col == N_COL - 1, (slice(None), pl.ds(width + LY, width)), side),
        ):
            @pl.when(missing)
            def _():
                ref[place] = jnp.zeros(shape, BF16)
    for a, b in COLS:
        @pl.when(jnp.logical_not(there[a, b]))
        def _():
            coarse[2, PLACE[b]] = jnp.zeros((RHS, MESSAGE), I16)

    def vec_copy(a, b):
        src, size, dst = halo_part(a, b, 1)
        k = RING1.index((a, b))
        return pltpu.make_async_remote_copy(
            src_ref=vecs.at[pl.ds(1 + src[0], size[0]), pl.ds(1 + src[1], size[1])],
            dst_ref=vecs.at[pl.ds(dst[0], size[0]), pl.ds(dst[1], size[1])],
            send_sem=vec_send.at[k], recv_sem=vec_recv.at[k], device_id=at(a, b), device_id_type=MESH,
        )

    def coef_copy(a, b):
        src, size, dst = halo_part(a, b, 2)
        k = RING1.index((a, b))
        return pltpu.make_async_remote_copy(
            src_ref=coef.at[pl.ds(2 + src[0], size[0]), pl.ds(2 + src[1], size[1])],
            dst_ref=coef.at[pl.ds(dst[0], size[0]), pl.ds(dst[1], size[1])],
            send_sem=coef_send.at[k], recv_sem=coef_recv.at[k], device_id=at(a, b), device_id_type=MESH,
        )

    def col_copy(a, b):
        place = PLACE[-b]
        return pltpu.make_async_remote_copy(
            src_ref=coarse.at[2, 0], dst_ref=coarse.at[2, place],
            send_sem=coarse_send.at[0, place], recv_sem=coarse_recv.at[0, place], device_id=at(a, b), device_id_type=MESH,
        )

    def row_copy(a, b):
        place = PLACE[-a]
        return pltpu.make_async_remote_copy(
            src_ref=coarse.at[2, 0], dst_ref=coarse.at[2 - a, 0],
            send_sem=coarse_send.at[1, place], recv_sem=coarse_recv.at[1, place], device_id=at(a, b), device_id_type=MESH,
        )

    def hand_on(side, a, b):
        place = PLACE[-a]
        pair = pl.ds(1 + 2 * side, 2)
        return pltpu.make_async_remote_copy(
            src_ref=coarse.at[2, pair], dst_ref=coarse.at[2 - a, pair],
            send_sem=coarse_send.at[2 + side, place], recv_sem=coarse_recv.at[2 + side, place],
            device_id=at(a, b), device_id_type=MESH,
        )

    has_side = (col > 0, col < N_COL - 1)

    def each_side(side, step):
        for a, b in ROWS:
            pl.when(there[a, b] & has_side[side])(functools.partial(step, side, a, b))

    load_vec.wait()
    load_leaf.wait()
    leaf = [(p // LY, p % LY) for p in range(LX * LY)]
    coeffs = [dot_t(vecs[1 + i, 1 + j], leafb[i, j]).astype(BF16) for i, j in leaf]
    for (i, j), value in zip(leaf, coeffs):
        coef[2 + i, 2 + j] = value
    load_cbasis.wait()
    load_ctr = pltpu.make_async_copy(ctrans_hbm, ctr, load_sem.at[3])
    load_near = []
    for p in range(LX * LY):
        load_near.append(pltpu.make_async_copy(near_hbm.at[p // LY, p % LY], nblk.at[p], near_sem.at[p]))
        load_near[-1].start()
        if p == 0:
            load_ctr.start()
    load_ftr = pltpu.make_async_copy(transfer_hbm, ftr, load_sem.at[4])
    load_ftr.start()
    own = sum(dot(value, cbasis[i, j]) for (i, j), value in zip(leaf, coeffs))
    coarse[2, 0] = encoded(own)

    above, below = jnp.minimum(row, 2), jnp.minimum(N_ROW - 1 - row, 2)
    ahead, behind = jnp.minimum(col, 2), jnp.minimum(N_COL - 1 - col, 2)
    pl.semaphore_wait(barrier, above + below + ahead + behind)

    each(SIDES[:2], lambda a, b: pl.semaphore_signal(ready, inc=1, device_id=at(a, b), device_id_type=MESH))
    each(COLS, lambda a, b: col_copy(a, b).start())
    each(ROWS, lambda a, b: row_copy(a, b).start())
    each(SIDES, lambda a, b: vec_copy(a, b).start())
    each(SIDES, lambda a, b: coef_copy(a, b).start())
    pl.semaphore_wait(ready, jnp.minimum(row, 1) + jnp.minimum(N_ROW - 1 - row, 1))
    each(CORNERS, lambda a, b: vec_copy(a, b).start())
    each(CORNERS, lambda a, b: coef_copy(a, b).start())

    for copy in load_small:
        copy.wait()
    for o, (a, b) in enumerate(FAR_OFFSETS):
        ring = [x for x in FAR_OFFSETS if (max(abs(x[0]), abs(x[1])) == 1) == (max(abs(a), abs(b)) == 1)].index((a, b))
        for p in range(LX * LY):
            i, j = p // LY, p % LY
            if max(abs(a), abs(b)) == 1:
                w = 1 - near_mask[i, j, ring]
            else:
                w = far_mask[i, j, ring]
            weights[o, p] = jnp.full((RHS, RANK), w.astype(F32), F32).astype(BF16)

    def near_term(p, s):
        i, j = p // LY, p % LY
        a, b = NEAR_OFFSETS[s]
        lhs = vecs[1 + i + a, 1 + j + b]
        if s != 4:
            live = near_mask[i, j, s if s < 4 else s - 1]
            lhs = lhs * jnp.full((RHS, LEAF), live.astype(F32), F32).astype(BF16)
        return dot(lhs, nblk[p, s])

    def inside(p, s):
        a, b = NEAR_OFFSETS[s]
        return 0 <= p // LY + a < LX and 0 <= p % LY + b < LY

    for p in range(LX * LY):
        if p == NEAR_FIRST:
            for side in (0, 1):
                each([k for k in COLS if (k[1] > 0) == side], lambda a, b: col_copy(-a, -b).wait_recv())
                each_side(side, lambda side, a, b: hand_on(side, a, b).start())
        load_near[p].wait()
        near_acc[p] = sum(near_term(p, s) for s in range(9) if inside(p, s))

    load_ctr.wait()
    for f in range(FAR2):
        whole = ctr[f]
        hi = whole.astype(BF16)
        ctr_hi[f] = hi
        ctr_lo[f] = (whole - hi.astype(F32)).astype(BF16)

    each(RING1, lambda a, b: vec_copy(-a, -b).wait_recv())
    for p in range(LX * LY):
        outer = [s for s in range(9) if not inside(p, s)]
        if outer:
            near_acc[p] += sum(near_term(p, s) for s in outer)

    load_ftr.wait()
    each(RING1, lambda a, b: coef_copy(-a, -b).wait_recv())
    local = jnp.zeros((LX * LY * RHS, RANK), F32)
    for o, (a, b) in enumerate(FAR_OFFSETS):
        lhs = coef[2 + a : 2 + a + LX, 2 + b : 2 + b + LY].reshape(LX * LY, RHS, RANK) * weights[o]
        local += dot(lhs.reshape(LX * LY * RHS, RANK), ftr[o])

    each(RING1, lambda a, b: vec_copy(a, b).wait_send())
    each(RING1, lambda a, b: coef_copy(a, b).wait_send())
    each(COLS, lambda a, b: col_copy(a, b).wait_send())
    each(ROWS, lambda a, b: row_copy(a, b).wait_send())
    each(ROWS, lambda a, b: row_copy(-a, -b).wait_recv())
    for side in (0, 1):
        each_side(side, lambda side, a, b: hand_on(side, -a, -b).wait_recv())

    total = jnp.zeros((RHS, COARSE), F32)
    both = jnp.zeros((2 * RHS, COARSE), F32)
    for f in range(FAR2):
        listed = clist[0, f]
        step_b = listed % N_COL - col
        place = jnp.where(step_b == 0, 0, jnp.where(step_b < 0, step_b + 3, step_b + 2))
        whole = decoded(coarse[jnp.clip(listed // N_COL - row + 2, 0, 4), jnp.clip(place, 0, 4)])
        hi = whole.astype(BF16)
        lo = (whole - hi.astype(F32)).astype(BF16)
        both += dot(jnp.concatenate([hi, lo], axis=0), ctr_hi[f])
        total += dot(hi, ctr_lo[f])
    total = both[:RHS] + (both[RHS:] + total)
    coarse_local = total.astype(BF16)
    down = [dot_t(coarse_local, cbasis[p // LY, p % LY]) for p in range(LX * LY)]
    whole = [(local[p * RHS : (p + 1) * RHS] + down[p]).astype(BF16) for p in range(LX * LY)]
    far = [dot(whole[p], leafb[p // LY, p % LY]) for p in range(LX * LY)]
    applied = [near_acc[p] + far[p] for p in range(LX * LY)]
    for p in range(LX * LY):
        out_ref[p // LY, p % LY] = applied[p]

    for side in (0, 1):
        each_side(side, lambda side, a, b: hand_on(side, a, b).wait_send())


def per_device(vectors, near_blocks, near_mask, far_mask, leaf_basis, far_transfer, coarse_basis, coarse_list, coarse_transfer):
    any_ = pl.BlockSpec(memory_space=pltpu.HBM)
    vmem = pl.BlockSpec(memory_space=pltpu.VMEM)
    dma = pltpu.SemaphoreType.DMA
    operands = [
        pltpu.with_memory_space_constraint(x, pltpu.HBM)
        for x in (
            vectors, near_blocks, near_mask, far_mask, leaf_basis.swapaxes(2, 3), far_transfer, coarse_basis, coarse_list,
            coarse_transfer[0],
        )
    ]
    return pl.pallas_call(
        kernel,
        out_shape=jax.ShapeDtypeStruct((LX, LY, RHS, LEAF), F32),
        in_specs=[any_] * 9,
        out_specs=vmem,
        scratch_shapes=[
            pltpu.VMEM((LX + 2, LY + 2, RHS, LEAF), BF16),
            pltpu.VMEM((LX + 4, LY + 4, RHS, RANK), BF16),
            pltpu.VMEM((5, 5, RHS, MESSAGE), I16),
            pltpu.VMEM((LX * LY, 9, LEAF, LEAF), BF16),
            pltpu.VMEM((LX, LY, RANK, LEAF), BF16),
            pltpu.VMEM((24, RANK, RANK), BF16),
            pltpu.VMEM((LX, LY, RANK, COARSE), BF16),
            pltpu.VMEM((FAR2, COARSE, COARSE), F32),
            pltpu.VMEM((FAR2, COARSE, COARSE), BF16),
            pltpu.VMEM((FAR2, COARSE, COARSE), BF16),
            pltpu.VMEM((LX * LY, RHS, LEAF), F32),
            pltpu.VMEM((24, LX * LY, RHS, RANK), BF16),
            pltpu.SMEM((LX, LY, 8), jnp.int32),
            pltpu.SMEM((LX, LY, 16), jnp.int32),
            pltpu.SMEM((1, FAR2), jnp.int32),
            dma((LX * LY,)),
            dma((8,)),
            dma((8,)),
            dma((8,)),
            dma((8,)),
            dma((8,)),
            dma((4, 5)),
            dma((4, 5)),
            pltpu.SemaphoreType.REGULAR,
        ],
        compiler_params=pltpu.CompilerParams(
            collective_id=0, has_side_effects=True, vmem_limit_bytes=40 * 1024 * 1024
        ),
    )(*operands)


def solution(mesh):
    placed = (
        P("row", "col", None, None),
        P("row", "col", None, None, None),
        P("row", "col", None),
        P("row", "col", None),
        P("row", "col", None, None),
        P(),
        P("row", "col", None, None),
        P(("row", "col"), None),
        P(("row", "col"), None, None, None),
    )
    return jax.shard_map(
        per_device, mesh=mesh, in_specs=placed, out_specs=P("row", "col", None, None), check_vma=False
    )
```

```python
import functools

import jax
import jax.numpy as jnp
from jax import lax
from jax.experimental import pallas as pl
from jax.experimental.pallas import tpu as pltpu
from jax.sharding import PartitionSpec as P

MESH = pl.DeviceIdType.MESH
LX, LY, RHS, LEAF, RANK, COARSE, FAR2 = 4, 2, 16, 256, 64, 256, 8
N_ROW, N_COL = 8, 16
NEAR_OFFSETS = [(a, b) for a in (-1, 0, 1) for b in (-1, 0, 1)]
FAR_OFFSETS = [(a, b) for a in range(-2, 3) for b in range(-2, 3) if (a, b) != (0, 0)]
RING1 = [(a, b) for a, b in NEAR_OFFSETS if (a, b) != (0, 0)]
COLS = [(0, -2), (0, 2), (0, 1), (0, -1)]
ROWS = [(-1, 0), (-2, 0), (2, 0), (1, 0)]
CORNERS = [(-1, -1), (-1, 1), (1, -1), (1, 1)]
PARTNERS = [(-1, 0), (-2, 0), (0, -2), (0, -1), (0, 2), (0, 1), (1, 0), (2, 0)]
SIDES = [(-1, 0), (1, 0), (0, -1), (0, 1)]
NEAR_FIRST = 3
PLACE = {0: 0, -2: 1, -1: 2, 1: 3, 2: 4}
BF16, F32, I16, I32 = jnp.bfloat16, jnp.float32, jnp.int16, jnp.int32
MESSAGE = COARSE + 128
LEAST = 2.0**-100


def dot(lhs, rhs):
    return lax.dot_general(lhs, rhs, (((1,), (0,)), ((), ())), preferred_element_type=F32)


def dot_t(lhs, rhs):
    return lax.dot_general(lhs, rhs, (((1,), (1,)), ((), ())), preferred_element_type=F32)


def halo_part(a, b, width):
    src, size, dst = [], [], []
    for step, own in ((a, LX), (b, LY)):
        size.append(own if step == 0 else width)
        src.append(own - width if step == 1 else 0)
        dst.append({-1: width + own, 0: width, 1: 0}[step])
    return src, size, dst


def encoded(values):
    largest = jnp.max(jnp.abs(values), axis=1, keepdims=True)
    exponent = jnp.floor(jnp.log2(jnp.maximum(largest, LEAST))) + 1.0
    whole = jnp.clip(jnp.round(values * jnp.exp2(15.0 - exponent)), -32767.0, 32767.0)
    tail = jnp.broadcast_to(exponent, (RHS, MESSAGE - COARSE))
    return jnp.concatenate([whole, tail], axis=1).astype(I32).astype(I16)


def decoded(message):
    numbers = message.astype(I32).astype(F32)
    scale = jnp.exp2(numbers[:, COARSE:] - 15.0)
    return numbers[:, :COARSE] * jnp.concatenate([scale] * (COARSE // scale.shape[1]), axis=1)


def kernel(
    vec_hbm, near_hbm, near_mask_hbm, far_mask_hbm, leaf_hbm, transfer_hbm, cbasis_hbm, clist_hbm, ctrans_hbm,
    out_ref,
    vecs, coef, coarse, nblk, leafb, ftr, cbasis, ctr, ctr_hi, ctr_lo, near_acc, weights,
    near_mask, far_mask, clist,
    near_sem, load_sem, vec_send, vec_recv, coef_send, coef_recv, coarse_send, coarse_recv, ready,
):
    row = lax.axis_index("row")
    col = lax.axis_index("col")

    def at(a, b):
        return (row + a, col + b)

    there = {}
    for a, b in PARTNERS + CORNERS:
        r, c = at(a, b)
        there[a, b] = (r >= 0) & (r < N_ROW) & (c >= 0) & (c < N_COL)

    def each(offsets, step):
        for a, b in offsets:
            pl.when(there[a, b])(functools.partial(step, a, b))

    barrier = pltpu.get_barrier_semaphore()
    each(PARTNERS, lambda a, b: pl.semaphore_signal(barrier, inc=1, device_id=at(a, b), device_id_type=MESH))

    load_vec = pltpu.make_async_copy(vec_hbm, vecs.at[pl.ds(1, LX), pl.ds(1, LY)], load_sem.at[2])
    load_vec.start()
    load_leaf = pltpu.make_async_copy(leaf_hbm, leafb, load_sem.at[0])
    load_leaf.start()
    load_cbasis = pltpu.make_async_copy(cbasis_hbm, cbasis, load_sem.at[1])
    load_cbasis.start()

    load_small = []
    for k, (src, dst) in enumerate(((near_mask_hbm, near_mask), (far_mask_hbm, far_mask), (clist_hbm, clist))):
        load_small.append(pltpu.make_async_copy(src, dst, load_sem.at[5 + k]))
        load_small[-1].start()
    for ref, width, last in ((vecs, 1, LEAF), (coef, 2, RANK)):
        edge = (width, LY + 2 * width, RHS, last)
        side = (LX + 2 * width, width, RHS, last)
        for missing, place, shape in (
            (row == 0, (pl.ds(0, width),), edge),
            (row == N_ROW - 1, (pl.ds(width + LX, width),), edge),
            (col == 0, (slice(None), pl.ds(0, width)), side),
            (col == N_COL - 1, (slice(None), pl.ds(width + LY, width)), side),
        ):
            @pl.when(missing)
            def _():
                ref[place] = jnp.zeros(shape, BF16)
    for a, b in COLS:
        @pl.when(jnp.logical_not(there[a, b]))
        def _():
            coarse[2, PLACE[b]] = jnp.zeros((RHS, MESSAGE), I16)

    def vec_copy(a, b):
        src, size, dst = halo_part(a, b, 1)
        k = RING1.index((a, b))
        return pltpu.make_async_remote_copy(
            src_ref=vecs.at[pl.ds(1 + src[0], size[0]), pl.ds(1 + src[1], size[1])],
            dst_ref=vecs.at[pl.ds(dst[0], size[0]), pl.ds(dst[1], size[1])],
            send_sem=vec_send.at[k], recv_sem=vec_recv.at[k], device_id=at(a, b), device_id_type=MESH,
        )

    def coef_copy(a, b):
        src, size, dst = halo_part(a, b, 2)
        k = RING1.index((a, b))
        return pltpu.make_async_remote_copy(
            src_ref=coef.at[pl.ds(2 + src[0], size[0]), pl.ds(2 + src[1], size[1])],
            dst_ref=coef.at[pl.ds(dst[0], size[0]), pl.ds(dst[1], size[1])],
            send_sem=coef_send.at[k], recv_sem=coef_recv.at[k], device_id=at(a, b), device_id_type=MESH,
        )

    def col_copy(a, b):
        place = PLACE[-b]
        return pltpu.make_async_remote_copy(
            src_ref=coarse.at[2, 0], dst_ref=coarse.at[2, place],
            send_sem=coarse_send.at[0, place], recv_sem=coarse_recv.at[0, place], device_id=at(a, b), device_id_type=MESH,
        )

    def row_copy(a, b):
        place = PLACE[-a]
        return pltpu.make_async_remote_copy(
            src_ref=coarse.at[2, 0], dst_ref=coarse.at[2 - a, 0],
            send_sem=coarse_send.at[1, place], recv_sem=coarse_recv.at[1, place], device_id=at(a, b), device_id_type=MESH,
        )

    def hand_on(side, a, b):
        place = PLACE[-a]
        pair = pl.ds(1 + 2 * side, 2)
        return pltpu.make_async_remote_copy(
            src_ref=coarse.at[2, pair], dst_ref=coarse.at[2 - a, pair],
            send_sem=coarse_send.at[2 + side, place], recv_sem=coarse_recv.at[2 + side, place],
            device_id=at(a, b), device_id_type=MESH,
        )

    has_side = (col > 0, col < N_COL - 1)

    def each_side(side, step):
        for a, b in ROWS:
            pl.when(there[a, b] & has_side[side])(functools.partial(step, side, a, b))

    load_vec.wait()
    load_leaf.wait()
    leaf = [(p // LY, p % LY) for p in range(LX * LY)]
    coeffs = [dot_t(vecs[1 + i, 1 + j], leafb[i, j]).astype(BF16) for i, j in leaf]
    for (i, j), value in zip(leaf, coeffs):
        coef[2 + i, 2 + j] = value
    load_cbasis.wait()
    load_ctr = pltpu.make_async_copy(ctrans_hbm, ctr, load_sem.at[3])
    load_near = []
    for p in range(LX * LY):
        load_near.append(pltpu.make_async_copy(near_hbm.at[p // LY, p % LY], nblk.at[p], near_sem.at[p]))
        load_near[-1].start()
        if p == 0:
            load_ctr.start()
    load_ftr = pltpu.make_async_copy(transfer_hbm, ftr, load_sem.at[4])
    load_ftr.start()
    own = sum(dot(value, cbasis[i, j]) for (i, j), value in zip(leaf, coeffs))
    coarse[2, 0] = encoded(own)

    above, below = jnp.minimum(row, 2), jnp.minimum(N_ROW - 1 - row, 2)
    ahead, behind = jnp.minimum(col, 2), jnp.minimum(N_COL - 1 - col, 2)
    pl.semaphore_wait(barrier, above + below + ahead + behind)

    each(SIDES[:2], lambda a, b: pl.semaphore_signal(ready, inc=1, device_id=at(a, b), device_id_type=MESH))
    each(COLS, lambda a, b: col_copy(a, b).start())
    each(ROWS, lambda a, b: row_copy(a, b).start())
    each(SIDES, lambda a, b: vec_copy(a, b).start())
    each(SIDES, lambda a, b: coef_copy(a, b).start())
    pl.semaphore_wait(ready, jnp.minimum(row, 1) + jnp.minimum(N_ROW - 1 - row, 1))
    each(CORNERS, lambda a, b: vec_copy(a, b).start())
    each(CORNERS, lambda a, b: coef_copy(a, b).start())

    for copy in load_small:
        copy.wait()
    for o, (a, b) in enumerate(FAR_OFFSETS):
        ring = [x for x in FAR_OFFSETS if (max(abs(x[0]), abs(x[1])) == 1) == (max(abs(a), abs(b)) == 1)].index((a, b))
        for p in range(LX * LY):
            i, j = p // LY, p % LY
            if max(abs(a), abs(b)) == 1:
                w = 1 - near_mask[i, j, ring]
            else:
                w = far_mask[i, j, ring]
            weights[o, p] = jnp.full((RHS, RANK), w.astype(F32), F32).astype(BF16)

    def near_term(p, s):
        i, j = p // LY, p % LY
        a, b = NEAR_OFFSETS[s]
        lhs = vecs[1 + i + a, 1 + j + b]
        if s != 4:
            live = near_mask[i, j, s if s < 4 else s - 1]
            lhs = lhs * jnp.full((RHS, LEAF), live.astype(F32), F32).astype(BF16)
        return dot(lhs, nblk[p, s])

    def inside(p, s):
        a, b = NEAR_OFFSETS[s]
        return 0 <= p // LY + a < LX and 0 <= p % LY + b < LY

    for p in range(LX * LY):
        if p == NEAR_FIRST:
            for side in (1, 0):
                each([k for k in COLS if (k[1] > 0) == side], lambda a, b: col_copy(-a, -b).wait_recv())
                each_side(side, lambda side, a, b: hand_on(side, a, b).start())
        load_near[p].wait()
        near_acc[p] = sum(near_term(p, s) for s in range(9) if inside(p, s))

    load_ctr.wait()
    for f in range(FAR2):
        whole = ctr[f]
        hi = whole.astype(BF16)
        ctr_hi[f] = hi
        ctr_lo[f] = (whole - hi.astype(F32)).astype(BF16)

    each(RING1, lambda a, b: vec_copy(-a, -b).wait_recv())
    for p in range(LX * LY):
        outer = [s for s in range(9) if not inside(p, s)]
        if outer:
            near_acc[p] += sum(near_term(p, s) for s in outer)

    load_ftr.wait()
    each(RING1, lambda a, b: coef_copy(-a, -b).wait_recv())
    local = jnp.zeros((LX * LY * RHS, RANK), F32)
    for o, (a, b) in enumerate(FAR_OFFSETS):
        lhs = coef[2 + a : 2 + a + LX, 2 + b : 2 + b + LY].reshape(LX * LY, RHS, RANK) * weights[o]
        local += dot(lhs.reshape(LX * LY * RHS, RANK), ftr[o])

    each(RING1, lambda a, b: vec_copy(a, b).wait_send())
    each(RING1, lambda a, b: coef_copy(a, b).wait_send())
    each(COLS, lambda a, b: col_copy(a, b).wait_send())
    each(ROWS, lambda a, b: row_copy(a, b).wait_send())
    each(ROWS, lambda a, b: row_copy(-a, -b).wait_recv())
    for side in (1, 0):
        each_side(side, lambda side, a, b: hand_on(side, -a, -b).wait_recv())

    total = jnp.zeros((RHS, COARSE), F32)
    both = jnp.zeros((2 * RHS, COARSE), F32)
    for f in range(FAR2):
        listed = clist[0, f]
        step_b = listed % N_COL - col
        place = jnp.where(step_b == 0, 0, jnp.where(step_b < 0, step_b + 3, step_b + 2))
        whole = decoded(coarse[jnp.clip(listed // N_COL - row + 2, 0, 4), jnp.clip(place, 0, 4)])
        hi = whole.astype(BF16)
        lo = (whole - hi.astype(F32)).astype(BF16)
        both += dot(jnp.concatenate([hi, lo], axis=0), ctr_hi[f])
        total += dot(hi, ctr_lo[f])
    total = both[:RHS] + (both[RHS:] + total)
    coarse_local = total.astype(BF16)
    down = [dot_t(coarse_local, cbasis[p // LY, p % LY]) for p in range(LX * LY)]
    whole = [(local[p * RHS : (p + 1) * RHS] + down[p]).astype(BF16) for p in range(LX * LY)]
    far = [dot(whole[p], leafb[p // LY, p % LY]) for p in range(LX * LY)]
    applied = [near_acc[p] + far[p] for p in range(LX * LY)]
    for p in range(LX * LY):
        out_ref[p // LY, p % LY] = applied[p]

    for side in (0, 1):
        each_side(side, lambda side, a, b: hand_on(side, a, b).wait_send())


def per_device(vectors, near_blocks, near_mask, far_mask, leaf_basis, far_transfer, coarse_basis, coarse_list, coarse_transfer):
    any_ = pl.BlockSpec(memory_space=pltpu.HBM)
    vmem = pl.BlockSpec(memory_space=pltpu.VMEM)
    dma = pltpu.SemaphoreType.DMA
    operands = [
        pltpu.with_memory_space_constraint(x, pltpu.HBM)
        for x in (
            vectors, near_blocks, near_mask, far_mask, leaf_basis.swapaxes(2, 3), far_transfer, coarse_basis, coarse_list,
            coarse_transfer[0],
        )
    ]
    return pl.pallas_call(
        kernel,
        out_shape=jax.ShapeDtypeStruct((LX, LY, RHS, LEAF), F32),
        in_specs=[any_] * 9,
        out_specs=vmem,
        scratch_shapes=[
            pltpu.VMEM((LX + 2, LY + 2, RHS, LEAF), BF16),
            pltpu.VMEM((LX + 4, LY + 4, RHS, RANK), BF16),
            pltpu.VMEM((5, 5, RHS, MESSAGE), I16),
            pltpu.VMEM((LX * LY, 9, LEAF, LEAF), BF16),
            pltpu.VMEM((LX, LY, RANK, LEAF), BF16),
            pltpu.VMEM((24, RANK, RANK), BF16),
            pltpu.VMEM((LX, LY, RANK, COARSE), BF16),
            pltpu.VMEM((FAR2, COARSE, COARSE), F32),
            pltpu.VMEM((FAR2, COARSE, COARSE), BF16),
            pltpu.VMEM((FAR2, COARSE, COARSE), BF16),
            pltpu.VMEM((LX * LY, RHS, LEAF), F32),
            pltpu.VMEM((24, LX * LY, RHS, RANK), BF16),
            pltpu.SMEM((LX, LY, 8), jnp.int32),
            pltpu.SMEM((LX, LY, 16), jnp.int32),
            pltpu.SMEM((1, FAR2), jnp.int32),
            dma((LX * LY,)),
            dma((8,)),
            dma((8,)),
            dma((8,)),
            dma((8,)),
            dma((8,)),
            dma((4, 5)),
            dma((4, 5)),
            pltpu.SemaphoreType.REGULAR,
        ],
        compiler_params=pltpu.CompilerParams(
            collective_id=0, has_side_effects=True, vmem_limit_bytes=40 * 1024 * 1024
        ),
    )(*operands)


def solution(mesh):
    placed = (
        P("row", "col", None, None),
        P("row", "col", None, None, None),
        P("row", "col", None),
        P("row", "col", None),
        P("row", "col", None, None),
        P(),
        P("row", "col", None, None),
        P(("row", "col"), None),
        P(("row", "col"), None, None, None),
    )
    return jax.shard_map(
        per_device, mesh=mesh, in_specs=placed, out_specs=P("row", "col", None, None), check_vma=False
    )
```

```python
import functools

import jax
import jax.numpy as jnp
from jax import lax
from jax.experimental import pallas as pl
from jax.experimental.pallas import tpu as pltpu
from jax.sharding import PartitionSpec as P

MESH = pl.DeviceIdType.MESH
LX, LY, RHS, LEAF, RANK, COARSE, FAR2 = 4, 2, 16, 256, 64, 256, 8
N_ROW, N_COL = 8, 16
NEAR_OFFSETS = [(a, b) for a in (-1, 0, 1) for b in (-1, 0, 1)]
FAR_OFFSETS = [(a, b) for a in range(-2, 3) for b in range(-2, 3) if (a, b) != (0, 0)]
RING1 = [(a, b) for a, b in NEAR_OFFSETS if (a, b) != (0, 0)]
COLS = [(0, -2), (0, 2), (0, 1), (0, -1)]
ROWS = [(-1, 0), (-2, 0), (2, 0), (1, 0)]
CORNERS = [(-1, -1), (-1, 1), (1, -1), (1, 1)]
PARTNERS = [(-1, 0), (-2, 0), (0, -2), (0, -1), (0, 2), (0, 1), (1, 0), (2, 0)]
SIDES = [(-1, 0), (1, 0), (0, -1), (0, 1)]
NEAR_FIRST = 3
PLACE = {0: 0, -2: 1, -1: 2, 1: 3, 2: 4}
BF16, F32, I16, I32 = jnp.bfloat16, jnp.float32, jnp.int16, jnp.int32
MESSAGE = COARSE + 128
LEAST = 2.0**-100


def dot(lhs, rhs):
    return lax.dot_general(lhs, rhs, (((1,), (0,)), ((), ())), preferred_element_type=F32)


def dot_t(lhs, rhs):
    return lax.dot_general(lhs, rhs, (((1,), (1,)), ((), ())), preferred_element_type=F32)


def halo_part(a, b, width):
    src, size, dst = [], [], []
    for step, own in ((a, LX), (b, LY)):
        size.append(own if step == 0 else width)
        src.append(own - width if step == 1 else 0)
        dst.append({-1: width + own, 0: width, 1: 0}[step])
    return src, size, dst


def encoded(values):
    largest = jnp.max(jnp.abs(values), axis=1, keepdims=True)
    exponent = jnp.floor(jnp.log2(jnp.maximum(largest, LEAST))) + 1.0
    whole = jnp.clip(jnp.round(values * jnp.exp2(15.0 - exponent)), -32767.0, 32767.0)
    tail = jnp.broadcast_to(exponent, (RHS, MESSAGE - COARSE))
    return jnp.concatenate([whole, tail], axis=1).astype(I32).astype(I16)


def decoded(message):
    numbers = message.astype(I32).astype(F32)
    scale = jnp.exp2(numbers[:, COARSE:] - 15.0)
    return numbers[:, :COARSE] * jnp.concatenate([scale] * (COARSE // scale.shape[1]), axis=1)


def kernel(
    vec_hbm, near_hbm, near_mask_hbm, far_mask_hbm, leaf_hbm, transfer_hbm, cbasis_hbm, clist_hbm, ctrans_hbm,
    out_ref,
    vecs, coef, coarse, nblk, leafb, ftr, cbasis, ctr, ctr_hi, ctr_lo, near_acc, weights,
    near_mask, far_mask, clist,
    near_sem, load_sem, vec_send, vec_recv, coef_send, coef_recv, coarse_send, coarse_recv, ready,
):
    row = lax.axis_index("row")
    col = lax.axis_index("col")

    def at(a, b):
        return (row + a, col + b)

    there = {}
    for a, b in PARTNERS + CORNERS:
        r, c = at(a, b)
        there[a, b] = (r >= 0) & (r < N_ROW) & (c >= 0) & (c < N_COL)

    def each(offsets, step):
        for a, b in offsets:
            pl.when(there[a, b])(functools.partial(step, a, b))

    load_vec = pltpu.make_async_copy(vec_hbm, vecs.at[pl.ds(1, LX), pl.ds(1, LY)], load_sem.at[2])
    load_vec.start()
    load_leaf = pltpu.make_async_copy(leaf_hbm, leafb, load_sem.at[0])
    load_leaf.start()
    load_cbasis = pltpu.make_async_copy(cbasis_hbm, cbasis, load_sem.at[1])
    load_cbasis.start()

    barrier = pltpu.get_barrier_semaphore()
    each(PARTNERS, lambda a, b: pl.semaphore_signal(barrier, inc=1, device_id=at(a, b), device_id_type=MESH))

    load_small = []
    for k, (src, dst) in enumerate(((near_mask_hbm, near_mask), (far_mask_hbm, far_mask), (clist_hbm, clist))):
        load_small.append(pltpu.make_async_copy(src, dst, load_sem.at[5 + k]))
        load_small[-1].start()
    for ref, width, last in ((vecs, 1, LEAF), (coef, 2, RANK)):
        edge = (width, LY + 2 * width, RHS, last)
        side = (LX + 2 * width, width, RHS, last)
        for missing, place, shape in (
            (row == 0, (pl.ds(0, width),), edge),
            (row == N_ROW - 1, (pl.ds(width + LX, width),), edge),
            (col == 0, (slice(None), pl.ds(0, width)), side),
            (col == N_COL - 1, (slice(None), pl.ds(width + LY, width)), side),
        ):
            @pl.when(missing)
            def _():
                ref[place] = jnp.zeros(shape, BF16)
    for a, b in COLS:
        @pl.when(jnp.logical_not(there[a, b]))
        def _():
            coarse[2, PLACE[b]] = jnp.zeros((RHS, MESSAGE), I16)

    def vec_copy(a, b):
        src, size, dst = halo_part(a, b, 1)
        k = RING1.index((a, b))
        return pltpu.make_async_remote_copy(
            src_ref=vecs.at[pl.ds(1 + src[0], size[0]), pl.ds(1 + src[1], size[1])],
            dst_ref=vecs.at[pl.ds(dst[0], size[0]), pl.ds(dst[1], size[1])],
            send_sem=vec_send.at[k], recv_sem=vec_recv.at[k], device_id=at(a, b), device_id_type=MESH,
        )

    def coef_copy(a, b):
        src, size, dst = halo_part(a, b, 2)
        k = RING1.index((a, b))
        return pltpu.make_async_remote_copy(
            src_ref=coef.at[pl.ds(2 + src[0], size[0]), pl.ds(2 + src[1], size[1])],
            dst_ref=coef.at[pl.ds(dst[0], size[0]), pl.ds(dst[1], size[1])],
            send_sem=coef_send.at[k], recv_sem=coef_recv.at[k], device_id=at(a, b), device_id_type=MESH,
        )

    def col_copy(a, b):
        place = PLACE[-b]
        return pltpu.make_async_remote_copy(
            src_ref=coarse.at[2, 0], dst_ref=coarse.at[2, place],
            send_sem=coarse_send.at[0, place], recv_sem=coarse_recv.at[0, place], device_id=at(a, b), device_id_type=MESH,
        )

    def row_copy(a, b):
        place = PLACE[-a]
        return pltpu.make_async_remote_copy(
            src_ref=coarse.at[2, 0], dst_ref=coarse.at[2 - a, 0],
            send_sem=coarse_send.at[1, place], recv_sem=coarse_recv.at[1, place], device_id=at(a, b), device_id_type=MESH,
        )

    def hand_on(side, a, b):
        place = PLACE[-a]
        pair = pl.ds(1 + 2 * side, 2)
        return pltpu.make_async_remote_copy(
            src_ref=coarse.at[2, pair], dst_ref=coarse.at[2 - a, pair],
            send_sem=coarse_send.at[2 + side, place], recv_sem=coarse_recv.at[2 + side, place],
            device_id=at(a, b), device_id_type=MESH,
        )

    has_side = (col > 0, col < N_COL - 1)

    def each_side(side, step):
        for a, b in ROWS:
            pl.when(there[a, b] & has_side[side])(functools.partial(step, side, a, b))

    load_vec.wait()
    load_leaf.wait()
    leaf = [(p // LY, p % LY) for p in range(LX * LY)]
    coeffs = [dot_t(vecs[1 + i, 1 + j], leafb[i, j]).astype(BF16) for i, j in leaf]
    for (i, j), value in zip(leaf, coeffs):
        coef[2 + i, 2 + j] = value
    load_cbasis.wait()
    load_ctr = pltpu.make_async_copy(ctrans_hbm, ctr, load_sem.at[3])
    load_near = []
    for p in range(LX * LY):
        load_near.append(pltpu.make_async_copy(near_hbm.at[p // LY, p % LY], nblk.at[p], near_sem.at[p]))
        load_near[-1].start()
        if p == 0:
            load_ctr.start()
    load_ftr = pltpu.make_async_copy(transfer_hbm, ftr, load_sem.at[4])
    load_ftr.start()
    own = sum(dot(value, cbasis[i, j]) for (i, j), value in zip(leaf, coeffs))
    coarse[2, 0] = encoded(own)

    above, below = jnp.minimum(row, 2), jnp.minimum(N_ROW - 1 - row, 2)
    ahead, behind = jnp.minimum(col, 2), jnp.minimum(N_COL - 1 - col, 2)
    pl.semaphore_wait(barrier, above + below + ahead + behind)

    each(SIDES[:2], lambda a, b: pl.semaphore_signal(ready, inc=1, device_id=at(a, b), device_id_type=MESH))
    each(COLS, lambda a, b: col_copy(a, b).start())
    each(ROWS, lambda a, b: row_copy(a, b).start())
    each(SIDES, lambda a, b: vec_copy(a, b).start())
    each(SIDES, lambda a, b: coef_copy(a, b).start())
    pl.semaphore_wait(ready, jnp.minimum(row, 1) + jnp.minimum(N_ROW - 1 - row, 1))
    each(CORNERS, lambda a, b: vec_copy(a, b).start())
    each(CORNERS, lambda a, b: coef_copy(a, b).start())

    for copy in load_small:
        copy.wait()
    for o, (a, b) in enumerate(FAR_OFFSETS):
        ring = [x for x in FAR_OFFSETS if (max(abs(x[0]), abs(x[1])) == 1) == (max(abs(a), abs(b)) == 1)].index((a, b))
        for p in range(LX * LY):
            i, j = p // LY, p % LY
            if max(abs(a), abs(b)) == 1:
                w = 1 - near_mask[i, j, ring]
            else:
                w = far_mask[i, j, ring]
            weights[o, p] = jnp.full((RHS, RANK), w.astype(F32), F32).astype(BF16)

    def near_term(p, s):
        i, j = p // LY, p % LY
        a, b = NEAR_OFFSETS[s]
        lhs = vecs[1 + i + a, 1 + j + b]
        if s != 4:
            live = near_mask[i, j, s if s < 4 else s - 1]
            lhs = lhs * jnp.full((RHS, LEAF), live.astype(F32), F32).astype(BF16)
        return dot(lhs, nblk[p, s])

    def inside(p, s):
        a, b = NEAR_OFFSETS[s]
        return 0 <= p // LY + a < LX and 0 <= p % LY + b < LY

    for p in range(LX * LY):
        if p == NEAR_FIRST:
            for side in (1, 0):
                each([k for k in COLS if (k[1] > 0) == side], lambda a, b: col_copy(-a, -b).wait_recv())
                each_side(side, lambda side, a, b: hand_on(side, a, b).start())
        load_near[p].wait()
        near_acc[p] = sum(near_term(p, s) for s in range(9) if inside(p, s))

    load_ctr.wait()
    for f in range(FAR2):
        whole = ctr[f]
        hi = whole.astype(BF16)
        ctr_hi[f] = hi
        ctr_lo[f] = (whole - hi.astype(F32)).astype(BF16)

    each(RING1, lambda a, b: vec_copy(-a, -b).wait_recv())
    for p in range(LX * LY):
        outer = [s for s in range(9) if not inside(p, s)]
        if outer:
            near_acc[p] += sum(near_term(p, s) for s in outer)

    load_ftr.wait()
    each(RING1, lambda a, b: coef_copy(-a, -b).wait_recv())
    local = jnp.zeros((LX * LY * RHS, RANK), F32)
    for o, (a, b) in enumerate(FAR_OFFSETS):
        lhs = coef[2 + a : 2 + a + LX, 2 + b : 2 + b + LY].reshape(LX * LY, RHS, RANK) * weights[o]
        local += dot(lhs.reshape(LX * LY * RHS, RANK), ftr[o])

    each(RING1, lambda a, b: vec_copy(a, b).wait_send())
    each(RING1, lambda a, b: coef_copy(a, b).wait_send())
    each(COLS, lambda a, b: col_copy(a, b).wait_send())
    each(ROWS, lambda a, b: row_copy(a, b).wait_send())
    each(ROWS, lambda a, b: row_copy(-a, -b).wait_recv())
    for side in (1, 0):
        each_side(side, lambda side, a, b: hand_on(side, -a, -b).wait_recv())

    total = jnp.zeros((RHS, COARSE), F32)
    both = jnp.zeros((2 * RHS, COARSE), F32)
    for f in range(FAR2):
        listed = clist[0, f]
        step_b = listed % N_COL - col
        place = jnp.where(step_b == 0, 0, jnp.where(step_b < 0, step_b + 3, step_b + 2))
        whole = decoded(coarse[jnp.clip(listed // N_COL - row + 2, 0, 4), jnp.clip(place, 0, 4)])
        hi = whole.astype(BF16)
        lo = (whole - hi.astype(F32)).astype(BF16)
        both += dot(jnp.concatenate([hi, lo], axis=0), ctr_hi[f])
        total += dot(hi, ctr_lo[f])
    total = both[:RHS] + (both[RHS:] + total)
    coarse_local = total.astype(BF16)
    down = [dot_t(coarse_local, cbasis[p // LY, p % LY]) for p in range(LX * LY)]
    whole = [(local[p * RHS : (p + 1) * RHS] + down[p]).astype(BF16) for p in range(LX * LY)]
    far = [dot(whole[p], leafb[p // LY, p % LY]) for p in range(LX * LY)]
    applied = [near_acc[p] + far[p] for p in range(LX * LY)]
    for p in range(LX * LY):
        out_ref[p // LY, p % LY] = applied[p]

    for side in (0, 1):
        each_side(side, lambda side, a, b: hand_on(side, a, b).wait_send())


def per_device(vectors, near_blocks, near_mask, far_mask, leaf_basis, far_transfer, coarse_basis, coarse_list, coarse_transfer):
    any_ = pl.BlockSpec(memory_space=pltpu.HBM)
    vmem = pl.BlockSpec(memory_space=pltpu.VMEM)
    dma = pltpu.SemaphoreType.DMA
    operands = [
        pltpu.with_memory_space_constraint(x, pltpu.HBM)
        for x in (
            vectors, near_blocks, near_mask, far_mask, leaf_basis.swapaxes(2, 3), far_transfer, coarse_basis, coarse_list,
            coarse_transfer[0],
        )
    ]
    return pl.pallas_call(
        kernel,
        out_shape=jax.ShapeDtypeStruct((LX, LY, RHS, LEAF), F32),
        in_specs=[any_] * 9,
        out_specs=vmem,
        scratch_shapes=[
            pltpu.VMEM((LX + 2, LY + 2, RHS, LEAF), BF16),
            pltpu.VMEM((LX + 4, LY + 4, RHS, RANK), BF16),
            pltpu.VMEM((5, 5, RHS, MESSAGE), I16),
            pltpu.VMEM((LX * LY, 9, LEAF, LEAF), BF16),
            pltpu.VMEM((LX, LY, RANK, LEAF), BF16),
            pltpu.VMEM((24, RANK, RANK), BF16),
            pltpu.VMEM((LX, LY, RANK, COARSE), BF16),
            pltpu.VMEM((FAR2, COARSE, COARSE), F32),
            pltpu.VMEM((FAR2, COARSE, COARSE), BF16),
            pltpu.VMEM((FAR2, COARSE, COARSE), BF16),
            pltpu.VMEM((LX * LY, RHS, LEAF), F32),
            pltpu.VMEM((24, LX * LY, RHS, RANK), BF16),
            pltpu.SMEM((LX, LY, 8), jnp.int32),
            pltpu.SMEM((LX, LY, 16), jnp.int32),
            pltpu.SMEM((1, FAR2), jnp.int32),
            dma((LX * LY,)),
            dma((8,)),
            dma((8,)),
            dma((8,)),
            dma((8,)),
            dma((8,)),
            dma((4, 5)),
            dma((4, 5)),
            pltpu.SemaphoreType.REGULAR,
        ],
        compiler_params=pltpu.CompilerParams(
            collective_id=0, has_side_effects=True, vmem_limit_bytes=40 * 1024 * 1024
        ),
    )(*operands)


def solution(mesh):
    placed = (
        P("row", "col", None, None),
        P("row", "col", None, None, None),
        P("row", "col", None),
        P("row", "col", None),
        P("row", "col", None, None),
        P(),
        P("row", "col", None, None),
        P(("row", "col"), None),
        P(("row", "col"), None, None, None),
    )
    return jax.shard_map(
        per_device, mesh=mesh, in_specs=placed, out_specs=P("row", "col", None, None), check_vma=False
    )
```

```python
import functools

import jax
import jax.numpy as jnp
from jax import lax
from jax.experimental import pallas as pl
from jax.experimental.pallas import tpu as pltpu
from jax.sharding import PartitionSpec as P

MESH = pl.DeviceIdType.MESH
LX, LY, RHS, LEAF, RANK, COARSE, FAR2 = 4, 2, 16, 256, 64, 256, 8
N_ROW, N_COL = 8, 16
NEAR_OFFSETS = [(a, b) for a in (-1, 0, 1) for b in (-1, 0, 1)]
FAR_OFFSETS = [(a, b) for a in range(-2, 3) for b in range(-2, 3) if (a, b) != (0, 0)]
RING1 = [(a, b) for a, b in NEAR_OFFSETS if (a, b) != (0, 0)]
COLS = [(0, -2), (0, 2), (0, 1), (0, -1)]
ROWS = [(-1, 0), (-2, 0), (1, 0), (2, 0)]
CORNERS = [(-1, -1), (-1, 1), (1, -1), (1, 1)]
PARTNERS = [(-1, 0), (-2, 0), (0, -2), (0, -1), (0, 2), (0, 1), (1, 0), (2, 0)]
SIDES = [(-1, 0), (1, 0), (0, -1), (0, 1)]
NEAR_FIRST = 3
PLACE = {0: 0, -2: 1, -1: 2, 1: 3, 2: 4}
BF16, F32, I16, I32 = jnp.bfloat16, jnp.float32, jnp.int16, jnp.int32
MESSAGE = COARSE + 128
LEAST = 2.0**-100


def dot(lhs, rhs):
    return lax.dot_general(lhs, rhs, (((1,), (0,)), ((), ())), preferred_element_type=F32)


def dot_t(lhs, rhs):
    return lax.dot_general(lhs, rhs, (((1,), (1,)), ((), ())), preferred_element_type=F32)


def halo_part(a, b, width):
    src, size, dst = [], [], []
    for step, own in ((a, LX), (b, LY)):
        size.append(own if step == 0 else width)
        src.append(own - width if step == 1 else 0)
        dst.append({-1: width + own, 0: width, 1: 0}[step])
    return src, size, dst


def encoded(values):
    largest = jnp.max(jnp.abs(values), axis=1, keepdims=True)
    exponent = jnp.floor(jnp.log2(jnp.maximum(largest, LEAST))) + 1.0
    whole = jnp.clip(jnp.round(values * jnp.exp2(15.0 - exponent)), -32767.0, 32767.0)
    tail = jnp.broadcast_to(exponent, (RHS, MESSAGE - COARSE))
    return jnp.concatenate([whole, tail], axis=1).astype(I32).astype(I16)


def decoded(message):
    numbers = message.astype(I32).astype(F32)
    scale = jnp.exp2(numbers[:, COARSE:] - 15.0)
    return numbers[:, :COARSE] * jnp.concatenate([scale] * (COARSE // scale.shape[1]), axis=1)


def kernel(
    vec_hbm, near_hbm, near_mask_hbm, far_mask_hbm, leaf_hbm, transfer_hbm, cbasis_hbm, clist_hbm, ctrans_hbm,
    out_ref,
    vecs, coef, coarse, nblk, leafb, ftr, cbasis, ctr, ctr_hi, ctr_lo, near_acc, weights,
    near_mask, far_mask, clist,
    near_sem, load_sem, vec_send, vec_recv, coef_send, coef_recv, coarse_send, coarse_recv, ready,
):
    row = lax.axis_index("row")
    col = lax.axis_index("col")

    def at(a, b):
        return (row + a, col + b)

    there = {}
    for a, b in PARTNERS + CORNERS:
        r, c = at(a, b)
        there[a, b] = (r >= 0) & (r < N_ROW) & (c >= 0) & (c < N_COL)

    def each(offsets, step):
        for a, b in offsets:
            pl.when(there[a, b])(functools.partial(step, a, b))

    barrier = pltpu.get_barrier_semaphore()
    each(PARTNERS, lambda a, b: pl.semaphore_signal(barrier, inc=1, device_id=at(a, b), device_id_type=MESH))

    load_vec = pltpu.make_async_copy(vec_hbm, vecs.at[pl.ds(1, LX), pl.ds(1, LY)], load_sem.at[2])
    load_vec.start()
    load_leaf = pltpu.make_async_copy(leaf_hbm, leafb, load_sem.at[0])
    load_leaf.start()
    load_cbasis = pltpu.make_async_copy(cbasis_hbm, cbasis, load_sem.at[1])
    load_cbasis.start()

    load_small = []
    for k, (src, dst) in enumerate(((near_mask_hbm, near_mask), (far_mask_hbm, far_mask), (clist_hbm, clist))):
        load_small.append(pltpu.make_async_copy(src, dst, load_sem.at[5 + k]))
        load_small[-1].start()
    for ref, width, last in ((vecs, 1, LEAF), (coef, 2, RANK)):
        edge = (width, LY + 2 * width, RHS, last)
        side = (LX + 2 * width, width, RHS, last)
        for missing, place, shape in (
            (row == 0, (pl.ds(0, width),), edge),
            (row == N_ROW - 1, (pl.ds(width + LX, width),), edge),
            (col == 0, (slice(None), pl.ds(0, width)), side),
            (col == N_COL - 1, (slice(None), pl.ds(width + LY, width)), side),
        ):
            @pl.when(missing)
            def _():
                ref[place] = jnp.zeros(shape, BF16)
    for a, b in COLS:
        @pl.when(jnp.logical_not(there[a, b]))
        def _():
            coarse[2, PLACE[b]] = jnp.zeros((RHS, MESSAGE), I16)

    def vec_copy(a, b):
        src, size, dst = halo_part(a, b, 1)
        k = RING1.index((a, b))
        return pltpu.make_async_remote_copy(
            src_ref=vecs.at[pl.ds(1 + src[0], size[0]), pl.ds(1 + src[1], size[1])],
            dst_ref=vecs.at[pl.ds(dst[0], size[0]), pl.ds(dst[1], size[1])],
            send_sem=vec_send.at[k], recv_sem=vec_recv.at[k], device_id=at(a, b), device_id_type=MESH,
        )

    def coef_copy(a, b):
        src, size, dst = halo_part(a, b, 2)
        k = RING1.index((a, b))
        return pltpu.make_async_remote_copy(
            src_ref=coef.at[pl.ds(2 + src[0], size[0]), pl.ds(2 + src[1], size[1])],
            dst_ref=coef.at[pl.ds(dst[0], size[0]), pl.ds(dst[1], size[1])],
            send_sem=coef_send.at[k], recv_sem=coef_recv.at[k], device_id=at(a, b), device_id_type=MESH,
        )

    def col_copy(a, b):
        place = PLACE[-b]
        return pltpu.make_async_remote_copy(
            src_ref=coarse.at[2, 0], dst_ref=coarse.at[2, place],
            send_sem=coarse_send.at[0, place], recv_sem=coarse_recv.at[0, place], device_id=at(a, b), device_id_type=MESH,
        )

    def row_copy(a, b):
        place = PLACE[-a]
        return pltpu.make_async_remote_copy(
            src_ref=coarse.at[2, 0], dst_ref=coarse.at[2 - a, 0],
            send_sem=coarse_send.at[1, place], recv_sem=coarse_recv.at[1, place], device_id=at(a, b), device_id_type=MESH,
        )

    def hand_on(side, a, b):
        place = PLACE[-a]
        pair = pl.ds(1 + 2 * side, 2)
        return pltpu.make_async_remote_copy(
            src_ref=coarse.at[2, pair], dst_ref=coarse.at[2 - a, pair],
            send_sem=coarse_send.at[2 + side, place], recv_sem=coarse_recv.at[2 + side, place],
            device_id=at(a, b), device_id_type=MESH,
        )

    has_side = (col > 0, col < N_COL - 1)

    def each_side(side, step):
        for a, b in ROWS:
            pl.when(there[a, b] & has_side[side])(functools.partial(step, side, a, b))

    load_vec.wait()
    load_leaf.wait()
    leaf = [(p // LY, p % LY) for p in range(LX * LY)]
    coeffs = [dot_t(vecs[1 + i, 1 + j], leafb[i, j]).astype(BF16) for i, j in leaf]
    for (i, j), value in zip(leaf, coeffs):
        coef[2 + i, 2 + j] = value
    load_cbasis.wait()
    load_ctr = pltpu.make_async_copy(ctrans_hbm, ctr, load_sem.at[3])
    load_near = []
    for p in range(LX * LY):
        load_near.append(pltpu.make_async_copy(near_hbm.at[p // LY, p % LY], nblk.at[p], near_sem.at[p]))
        load_near[-1].start()
        if p == 0:
            load_ctr.start()
    load_ftr = pltpu.make_async_copy(transfer_hbm, ftr, load_sem.at[4])
    load_ftr.start()
    own = sum(dot(value, cbasis[i, j]) for (i, j), value in zip(leaf, coeffs))
    coarse[2, 0] = encoded(own)

    above, below = jnp.minimum(row, 2), jnp.minimum(N_ROW - 1 - row, 2)
    ahead, behind = jnp.minimum(col, 2), jnp.minimum(N_COL - 1 - col, 2)
    pl.semaphore_wait(barrier, above + below + ahead + behind)

    each(SIDES[:2], lambda a, b: pl.semaphore_signal(ready, inc=1, device_id=at(a, b), device_id_type=MESH))
    each(COLS, lambda a, b: col_copy(a, b).start())
    each(ROWS, lambda a, b: row_copy(a, b).start())
    each(SIDES, lambda a, b: vec_copy(a, b).start())
    each(SIDES, lambda a, b: coef_copy(a, b).start())
    pl.semaphore_wait(ready, jnp.minimum(row, 1) + jnp.minimum(N_ROW - 1 - row, 1))
    each(CORNERS, lambda a, b: vec_copy(a, b).start())
    each(CORNERS, lambda a, b: coef_copy(a, b).start())

    for copy in load_small:
        copy.wait()
    for o, (a, b) in enumerate(FAR_OFFSETS):
        ring = [x for x in FAR_OFFSETS if (max(abs(x[0]), abs(x[1])) == 1) == (max(abs(a), abs(b)) == 1)].index((a, b))
        for p in range(LX * LY):
            i, j = p // LY, p % LY
            if max(abs(a), abs(b)) == 1:
                w = 1 - near_mask[i, j, ring]
            else:
                w = far_mask[i, j, ring]
            weights[o, p] = jnp.full((RHS, RANK), w.astype(F32), F32).astype(BF16)

    def near_term(p, s):
        i, j = p // LY, p % LY
        a, b = NEAR_OFFSETS[s]
        lhs = vecs[1 + i + a, 1 + j + b]
        if s != 4:
            live = near_mask[i, j, s if s < 4 else s - 1]
            lhs = lhs * jnp.full((RHS, LEAF), live.astype(F32), F32).astype(BF16)
        return dot(lhs, nblk[p, s])

    def inside(p, s):
        a, b = NEAR_OFFSETS[s]
        return 0 <= p // LY + a < LX and 0 <= p % LY + b < LY

    for p in range(LX * LY):
        if p == NEAR_FIRST:
            for side in (1, 0):
                each([k for k in COLS if (k[1] > 0) == side], lambda a, b: col_copy(-a, -b).wait_recv())
                each_side(side, lambda side, a, b: hand_on(side, a, b).start())
        load_near[p].wait()
        near_acc[p] = sum(near_term(p, s) for s in range(9) if inside(p, s))

    load_ctr.wait()
    for f in range(FAR2):
        whole = ctr[f]
        hi = whole.astype(BF16)
        ctr_hi[f] = hi
        ctr_lo[f] = (whole - hi.astype(F32)).astype(BF16)

    each(RING1, lambda a, b: vec_copy(-a, -b).wait_recv())
    for p in range(LX * LY):
        outer = [s for s in range(9) if not inside(p, s)]
        if outer:
            near_acc[p] += sum(near_term(p, s) for s in outer)

    load_ftr.wait()
    each(RING1, lambda a, b: coef_copy(-a, -b).wait_recv())
    local = jnp.zeros((LX * LY * RHS, RANK), F32)
    for o, (a, b) in enumerate(FAR_OFFSETS):
        lhs = coef[2 + a : 2 + a + LX, 2 + b : 2 + b + LY].reshape(LX * LY, RHS, RANK) * weights[o]
        local += dot(lhs.reshape(LX * LY * RHS, RANK), ftr[o])

    each(RING1, lambda a, b: vec_copy(a, b).wait_send())
    each(RING1, lambda a, b: coef_copy(a, b).wait_send())
    each(COLS, lambda a, b: col_copy(a, b).wait_send())
    each(ROWS, lambda a, b: row_copy(a, b).wait_send())
    each(ROWS, lambda a, b: row_copy(-a, -b).wait_recv())
    for side in (1, 0):
        each_side(side, lambda side, a, b: hand_on(side, -a, -b).wait_recv())

    total = jnp.zeros((RHS, COARSE), F32)
    both = jnp.zeros((2 * RHS, COARSE), F32)
    for f in range(FAR2):
        listed = clist[0, f]
        step_b = listed % N_COL - col
        place = jnp.where(step_b == 0, 0, jnp.where(step_b < 0, step_b + 3, step_b + 2))
        whole = decoded(coarse[jnp.clip(listed // N_COL - row + 2, 0, 4), jnp.clip(place, 0, 4)])
        hi = whole.astype(BF16)
        lo = (whole - hi.astype(F32)).astype(BF16)
        both += dot(jnp.concatenate([hi, lo], axis=0), ctr_hi[f])
        total += dot(hi, ctr_lo[f])
    total = both[:RHS] + (both[RHS:] + total)
    coarse_local = total.astype(BF16)
    down = [dot_t(coarse_local, cbasis[p // LY, p % LY]) for p in range(LX * LY)]
    whole = [(local[p * RHS : (p + 1) * RHS] + down[p]).astype(BF16) for p in range(LX * LY)]
    far = [dot(whole[p], leafb[p // LY, p % LY]) for p in range(LX * LY)]
    applied = [near_acc[p] + far[p] for p in range(LX * LY)]
    for p in range(LX * LY):
        out_ref[p // LY, p % LY] = applied[p]

    for side in (0, 1):
        each_side(side, lambda side, a, b: hand_on(side, a, b).wait_send())


def per_device(vectors, near_blocks, near_mask, far_mask, leaf_basis, far_transfer, coarse_basis, coarse_list, coarse_transfer):
    any_ = pl.BlockSpec(memory_space=pltpu.HBM)
    vmem = pl.BlockSpec(memory_space=pltpu.VMEM)
    dma = pltpu.SemaphoreType.DMA
    operands = [
        pltpu.with_memory_space_constraint(x, pltpu.HBM)
        for x in (
            vectors, near_blocks, near_mask, far_mask, leaf_basis.swapaxes(2, 3), far_transfer, coarse_basis, coarse_list,
            coarse_transfer[0],
        )
    ]
    return pl.pallas_call(
        kernel,
        out_shape=jax.ShapeDtypeStruct((LX, LY, RHS, LEAF), F32),
        in_specs=[any_] * 9,
        out_specs=vmem,
        scratch_shapes=[
            pltpu.VMEM((LX + 2, LY + 2, RHS, LEAF), BF16),
            pltpu.VMEM((LX + 4, LY + 4, RHS, RANK), BF16),
            pltpu.VMEM((5, 5, RHS, MESSAGE), I16),
            pltpu.VMEM((LX * LY, 9, LEAF, LEAF), BF16),
            pltpu.VMEM((LX, LY, RANK, LEAF), BF16),
            pltpu.VMEM((24, RANK, RANK), BF16),
            pltpu.VMEM((LX, LY, RANK, COARSE), BF16),
            pltpu.VMEM((FAR2, COARSE, COARSE), F32),
            pltpu.VMEM((FAR2, COARSE, COARSE), BF16),
            pltpu.VMEM((FAR2, COARSE, COARSE), BF16),
            pltpu.VMEM((LX * LY, RHS, LEAF), F32),
            pltpu.VMEM((24, LX * LY, RHS, RANK), BF16),
            pltpu.SMEM((LX, LY, 8), jnp.int32),
            pltpu.SMEM((LX, LY, 16), jnp.int32),
            pltpu.SMEM((1, FAR2), jnp.int32),
            dma((LX * LY,)),
            dma((8,)),
            dma((8,)),
            dma((8,)),
            dma((8,)),
            dma((8,)),
            dma((4, 5)),
            dma((4, 5)),
            pltpu.SemaphoreType.REGULAR,
        ],
        compiler_params=pltpu.CompilerParams(
            collective_id=0, has_side_effects=True, vmem_limit_bytes=40 * 1024 * 1024
        ),
    )(*operands)


def solution(mesh):
    placed = (
        P("row", "col", None, None),
        P("row", "col", None, None, None),
        P("row", "col", None),
        P("row", "col", None),
        P("row", "col", None, None),
        P(),
        P("row", "col", None, None),
        P(("row", "col"), None),
        P(("row", "col"), None, None, None),
    )
    return jax.shard_map(
        per_device, mesh=mesh, in_specs=placed, out_specs=P("row", "col", None, None), check_vma=False
    )
```
